128 devices in a mesh: rep: 32 (over y, x, z_hi), shard: 4 (over z_lo, core).
Axes of the slice: x: 4, y: 4, z: 4 (z_hi: 2, z_lo: 2; z = z_hi * 2 + z_lo), core: 2. Of those that a mesh axis runs over, the one named last changes fastest.
Arguments:
- partials: bfloat16 [32, 4, 192, 28672], P('rep', 'shard'), may hold values from -6 to 6
- momentum: float32 [32, 192, 28672], P('rep', None, 'shard'), may hold values from -6 to 6
- weight: bfloat16 [192, 28672], P(None, 'shard'), may hold values from -6 to 6
- kept: int32 [6, 896, 64], P(None, 'shard'), may hold values from 0 to 495, as said below
Outputs:
- new_momentum: float32 [32, 192, 28672], P('rep', None, 'shard')
- aggregate: float32 [192, 28672], P(None, 'shard')
- new_weight: bfloat16 [192, 28672], P(None, 'shard')
The draws below stay inside these ranges and needn't reach their ends.
Inputs may be any that keep to these rules, and one draw needn't show every extreme that they name: `kept`: within each block the 64 positions are distinct, and each is 32 k + l with k and l below 16 (the positions are fixed in advance and shared by all replicas, a simplification of DeMo's per-replica top-k).
All inputs are finite; a program needn't handle non-finite values.
Results may differ from the reference program's by a relative error of at most 0.001.
Values sent between devices are 32-bit elements; how exact they have to be, the bound alone decides.
A program may use at most 192 MiB of HBM per device.

```python
import jax
import jax.numpy as jnp
from jax import lax

FF = 28672
ROWS = 192
RB = 6
CB = 896
N_REP = 32
N_SHARD = 4


def draw_kept(key, part):
    key = jax.random.fold_in(key, 7)
    scores = jax.random.randint(key, (RB, CB, 256), 0, 2 ** 20) * 256 + jnp.arange(256, dtype=jnp.int32)
    corner = jnp.logical_or(jnp.arange(256) == 0, jnp.arange(256) == 255)
    first = jnp.logical_and(jnp.arange(RB)[:, None, None] == 0, jnp.arange(CB)[None, :, None] == 0)
    scores = scores + jnp.where(jnp.logical_and(first, corner[None, None, :]), 2 ** 30, 0).astype(jnp.int32)
    chosen = jax.lax.top_k(scores, 64)[1].astype(jnp.int32)
    return (chosen // 16 * 32 + chosen % 16).astype(jnp.int32)


def level_of(rng, extent, shards, least, top_value):
    loudness, own = 1.0, jax.random.fold_in(rng, 6)
    for axis_at, blocks in shards:
        draws = jnp.exp(jax.random.uniform(jax.random.fold_in(own, axis_at), (blocks,), jnp.float32, least / len(shards), top_value / len(shards)))
        loudness = loudness * jnp.repeat(draws, extent[axis_at] // blocks).reshape([-1 if axis == axis_at else 1 for axis in range(len(extent))])
    return loudness


def centred(own_key, shape, scale, reach, cuts=(), held_as=jnp.bfloat16):
    factor_of = level_of(own_key, shape, cuts, -0.22, 0.18) if cuts else 1.0
    array = jax.random.normal(own_key, shape, jnp.float32) * scale * factor_of
    return jnp.minimum(jnp.maximum(array, -reach), reach).astype(held_as)


def setup_inputs(seed: int = 0) -> dict:
    splits = jax.random.split(jax.random.key(seed), 5)
    return {
        "partials": centred(splits[0], (N_REP, N_SHARD, ROWS, FF), 1.0, 6.0, ((0, 32), (1, 4))),
        "momentum": centred(splits[1], (N_REP, ROWS, FF), 1.0, 6.0, ((0, 32), (2, 4)), jnp.float32),
        "weight": centred(splits[2], (ROWS, FF), 1.0, 6.0, ((1, 4),)),
        "kept": draw_kept(jax.random.fold_in(splits[4], 71), 0),
    }


decay_rate = 0.9
step_rate = 0.5

def dct_matrix():
    freq = jnp.arange(32, dtype=jnp.float32)[:, None]
    place_idx = jnp.arange(32, dtype=jnp.float32)[None, :]
    table = jnp.cos(jnp.pi * (2.0 * place_idx + 1.0) * freq / 64.0) * jnp.sqrt(jnp.float32(2.0 / 32.0))
    return jnp.where(freq == 0.0, table * jnp.sqrt(jnp.float32(0.5)), table)

def forward(band_data, table, block_table):
    lefted = jnp.einsum('ki,biw->bkw', table, band_data, precision=lax.Precision.HIGHEST)
    count, height, width_cols = lefted.shape
    righted = jnp.dot(lefted.reshape(-1, 128), block_table, precision=lax.Precision.HIGHEST)
    return righted.reshape(count, height * width_cols)

def inverse(flat_coeffs, table, block_table, width_cols):
    count = flat_coeffs.shape[0]
    righted = jnp.dot(flat_coeffs.reshape(-1, 128), block_table.T, precision=lax.Precision.HIGHEST)
    lefted = righted.reshape(count, 32, width_cols)
    return jnp.einsum('ki,bkw->biw', table, lefted, precision=lax.Precision.HIGHEST)

def positions(kept, width_cols):
    count, blocks, keep_count = kept.shape
    column_base = (jnp.arange(blocks, dtype=jnp.int32) * 32)[None, :, None]
    flat_pos = kept // 32 * width_cols + column_base + kept % 32
    return flat_pos.reshape(count, blocks * keep_count).astype(jnp.int32)

def place_values(values, flat_pos, total):
    count = values.shape[0]
    band_rows = jnp.arange(count, dtype=jnp.int32)[:, None]
    return jnp.zeros((count, total), jnp.float32).at[band_rows, flat_pos].set(values)

def reference(partials, momentum, weight, kept):
    table = dct_matrix()
    block_table = jnp.kron(jnp.eye(4, dtype=jnp.float32), table.T)
    total_rows, width_cols = weight.shape
    band_count = total_rows // 32
    flat_pos = positions(kept, width_cols)

    def one_replica(pair):
        parts, moment_in = pair
        grad = lax.optimization_barrier(jnp.sum(parts.astype(jnp.float32), axis=0))
        moment = decay_rate * moment_in + grad
        band_data = moment.reshape(band_count, 32, width_cols)
        coeffs = forward(band_data, table, block_table)
        sent = jnp.take_along_axis(coeffs, flat_pos, axis=1)
        estimate = inverse(place_values(sent, flat_pos, 32 * width_cols), table, block_table, width_cols)
        return (moment - estimate.reshape(total_rows, width_cols), sent)
    new_momentum, sent_all = lax.map(one_replica, (partials, momentum))
    mean_sent = lax.optimization_barrier(jnp.sum(sent_all, axis=0)) / sent_all.shape[0]
    aggregate = inverse(place_values(mean_sent, flat_pos, 32 * width_cols), table, block_table, width_cols)
    aggregate = aggregate.reshape(total_rows, width_cols)
    new_weight = (weight.astype(jnp.float32) - step_rate * aggregate).astype(jnp.bfloat16)
    return (new_momentum, aggregate, new_weight)
```

```python
import functools

import jax
import jax.numpy as jnp
import numpy as np
from jax import lax
from jax.experimental import pallas as pl
from jax.experimental.pallas import tpu as pltpu
from jax.sharding import PartitionSpec as P

decay_rate = 0.9
step_rate = 0.5

MESH = pl.DeviceIdType.MESH
ROWS = 192
LOW = 96
CHUNK = 512
CHUNKS = 14
GROUPS = 7
QUARTER = CHUNK * CHUNKS
SLOTS = 4
PIECE = 24


def low_tables():
    freq = np.arange(16, dtype=np.float64)[:, None]
    place = np.arange(32, dtype=np.float64)[None, :]
    low = np.cos(np.pi * (2.0 * place + 1.0) * freq / 64.0) * np.sqrt(2.0 / 32.0)
    low[0] *= np.sqrt(0.5)
    left = np.kron(np.eye(6), low)
    right = np.kron(np.eye(8), low.T)

    def split(table):
        table = table.astype(np.float32)
        high = table.astype(jnp.bfloat16)
        rest = (table - high.astype(np.float32)).astype(jnp.bfloat16)
        return np.stack([high, rest])

    return split(left), split(right), split(left.T.copy()), split(right.T.copy())


def split_dot(a, b):
    if isinstance(a, tuple):
        a_high, a_rest = a
        b_high = b.astype(jnp.bfloat16)
        b_rest = (b - b_high.astype(jnp.float32)).astype(jnp.bfloat16)
    else:
        b_high, b_rest = b
        a_high = a.astype(jnp.bfloat16)
        a_rest = (a - a_high.astype(jnp.float32)).astype(jnp.bfloat16)
    dot = functools.partial(jnp.dot, preferred_element_type=jnp.float32)
    return dot(a_high, b_high) + (dot(a_high, b_rest) + dot(a_rest, b_high))


def kernel(part, mom, wt, kept, left_in, right_in, left_t_in, right_t_in,
           moment_out, agg_out, weight_out,
           pbuf, stage, sib, zrecv, mombuf, wbuf, cf, rsr, red, z3r, mean, mask, keptb, rowbits,
           left, right, left_t, right_t,
           const_sem, p_sem, m_sem, w_sem, ss_sem, sr_sem, zs_sem, zr_sem,
           rs_s, rs_r, z3_s, z3_r, ag_s, ag_r, om_sem, oa_sem, ow_sem):
    f32 = jnp.float32
    rep, shard = lax.axis_index("rep"), lax.axis_index("shard")
    plane, z_hi = rep // 2, rep % 2
    y, x = plane // 4, plane % 4
    z_lo, core = shard // 2, shard % 2
    z = z_hi * 2 + z_lo

    def in_plane(k):
        py, px = (y + k // 4) % 4, (x + k % 4) % 4
        return py, px, ((py * 4 + px) * 2 + z_hi, shard)

    def along_z(dz):
        other = (z + dz) % 4
        return (plane * 2 + other // 2, (other % 2) * 2 + core)

    sibling = (rep, z_lo * 2 + (1 - core))
    partner = (rep, (1 - z_lo) * 2 + core)
    quarters = ((1 - z_lo) * 2 + (1 - core), z_lo * 2 + (1 - core), (1 - z_lo) * 2 + core, shard)

    def load_part(c):
        return [
            pltpu.make_async_copy(
                part.at[0, 0, :, pl.ds(pl.multiple_of(q * QUARTER + c * CHUNK, CHUNK), CHUNK)],
                pbuf.at[c, n], p_sem.at[c])
            for n, q in enumerate(quarters)
        ]

    def columns(c):
        return pl.ds(pl.multiple_of(c * CHUNK, CHUNK), CHUNK)

    def load_mom(c):
        return pltpu.make_async_copy(mom.at[0, :, columns(c)], mombuf.at[c], m_sem.at[c])

    def load_weight(c):
        return pltpu.make_async_copy(wt.at[:, columns(c)], wbuf.at[c], w_sem.at[c])

    consts = [
        pltpu.make_async_copy(src, dst, const_sem.at[n])
        for n, (src, dst) in enumerate(
            ((left_in, left), (right_in, right), (left_t_in, left_t), (right_t_in, right_t), (kept, keptb)))
    ]

    def start_part(c, carry):
        for copy in load_part(c):
            copy.start()
        return carry

    def start_rest(c, carry):
        load_mom(c).start()
        load_weight(c).start()
        return carry

    start_part(0, 0)
    for copy in consts:
        copy.start()
    lax.fori_loop(1, CHUNKS, start_part, 0)
    lax.fori_loop(0, CHUNKS, start_rest, 0)

    barrier = pltpu.get_barrier_semaphore()
    pl.semaphore_signal(barrier, inc=1, device_id=sibling, device_id_type=MESH)

    def greet(k, carry):
        pl.semaphore_signal(barrier, inc=1, device_id=in_plane(k)[2], device_id_type=MESH)
        return carry

    lax.fori_loop(1, 16, greet, 0)
    for dz in (1, 2, 3):
        pl.semaphore_signal(barrier, inc=1, device_id=along_z(dz), device_id_type=MESH)
    pl.semaphore_wait(barrier, 19)

    def forward(block):
        lefted = split_dot((left[0], left[1]), block)
        return split_dot(lefted, (right[0], right[1]))

    def inverse(low):
        wide = split_dot(low, (right_t[0], right_t[1]))
        return split_dot((left_t[0], left_t[1]), wide)

    def sib_copy(c, n):
        return pltpu.make_async_remote_copy(
            src_ref=stage.at[c % SLOTS, n], dst_ref=sib.at[n, c],
            send_sem=ss_sem.at[c % SLOTS, n], recv_sem=sr_sem.at[c, n],
            device_id=sibling, device_id_type=MESH)

    def z_copy(c):
        return pltpu.make_async_remote_copy(
            src_ref=sib.at[0, c], dst_ref=zrecv.at[c],
            send_sem=zs_sem.at[c], recv_sem=zr_sem.at[c],
            device_id=partner, device_id_type=MESH)

    def send_stage(c):
        pltpu.make_async_copy(pbuf.at[c], pbuf.at[c], p_sem.at[c]).wait()
        for n in (0, 1):
            @pl.when(c >= SLOTS)
            def _():
                sib_copy(c, n).wait_send()
            stage[c % SLOTS, n] = pbuf[c, n].astype(f32)
            sib_copy(c, n).start()

    def process(g, half):
        c = 2 * g + half
        sib_copy(c, 0).wait_recv()
        sib[0, c] = sib[0, c] + pbuf[c, 2].astype(f32)
        z_copy(c).start()
        for h in (0, 1):
            cf[g, 1, 2 * half + h] = forward(sib[0, c, :, 256 * h:256 * h + 256])
        sib_copy(c, 1).wait_recv()
        load_mom(c).wait()
        sib[1, c] = sib[1, c] + pbuf[c, 3].astype(f32) + decay_rate * mombuf[c]
        for h in (0, 1):
            cf[g, 0, 2 * half + h] = forward(sib[1, c, :, 256 * h:256 * h + 256])

    def rs_send(g):
        def one(k, carry):
            py, px, target = in_plane(k)
            pltpu.make_async_remote_copy(
                src_ref=cf.at[g, :, py, pl.ds(pl.multiple_of(px * PIECE, 8), PIECE)],
                dst_ref=rsr.at[g, k - 1],
                send_sem=rs_s.at[g], recv_sem=rs_r.at[g],
                device_id=target, device_id_type=MESH).start()
            return carry
        lax.fori_loop(1, 16, one, 0)

    send_stage(0)
    for copy in consts:
        copy.wait()

    def gather_chip(g, carry):
        send_stage(2 * g + 1)
        process(g, 0)

        @pl.when(g < GROUPS - 1)
        def _():
            send_stage(2 * g + 2)
        process(g, 1)
        rs_send(g)
        return carry

    lax.fori_loop(0, GROUPS, gather_chip, 0)

    def band_words(b, carry):
        at = jnp.transpose(keptb[b])
        row, word = at // 32, jnp.left_shift(jnp.ones_like(at), at % 32)
        for k in range(16):
            rowbits[b, pl.ds(k, 1), :] = jnp.sum(jnp.where(row == k, word, 0), axis=0, keepdims=True)
        return carry

    lax.fori_loop(0, 6, band_words, 0)

    def group_mask(g, carry):
        words = rowbits[...].reshape(LOW, 224)
        upper = (words // 256).astype(f32).astype(jnp.bfloat16)
        lower = (words % 256).astype(f32).astype(jnp.bfloat16)
        block = lax.broadcasted_iota(jnp.int32, (224, 128), 0)
        lane = lax.broadcasted_iota(jnp.int32, (224, 128), 1)
        bit = lax.broadcasted_iota(jnp.int32, (LOW, 128), 1) % 16
        for j in range(4):
            spread = (block == (g * 4 + j) * 8 + lane // 16).astype(f32).astype(jnp.bfloat16)
            high = jnp.dot(upper, spread, preferred_element_type=f32)
            low = jnp.dot(lower, spread, preferred_element_type=f32)
            word = (high * 256.0 + low).astype(jnp.int32)
            mask[g, j] = (jnp.right_shift(word, bit) & 1).astype(f32)
        return carry

    lax.fori_loop(0, GROUPS, group_mask, 0)

    mine = pl.ds(pl.multiple_of(x * PIECE, 8), PIECE)

    def z3_copy(g, dz):
        return pltpu.make_async_remote_copy(
            src_ref=red.at[g, dz % 2], dst_ref=z3r.at[g, dz - 1],
            send_sem=z3_s.at[g, dz - 1], recv_sem=z3_r.at[g, dz - 1],
            device_id=along_z(dz), device_id_type=MESH)

    def sum_plane(g, carry):
        pltpu.make_async_copy(rsr.at[g], rsr.at[g], rs_r.at[g]).wait()
        for n in (0, 1):
            total = cf[g, n, y, mine]
            for k in range(15):
                total = total + rsr[g, k, n]
            red[g, n] = total
        for dz in (1, 2, 3):
            z3_copy(g, dz).start()
        return carry

    lax.fori_loop(0, GROUPS, sum_plane, 0)

    def sum_z(g, carry):
        for dz in (1, 2, 3):
            z3_copy(g, dz).wait_recv()
        mean[g, y, mine] = red[g, 0] + (z3r[g, 0] + z3r[g, 1] + z3r[g, 2])

        def one(k, inner):
            target = in_plane(k)[2]
            pltpu.make_async_remote_copy(
                src_ref=mean.at[g, y, mine], dst_ref=mean.at[g, y, mine],
                send_sem=ag_s.at[g], recv_sem=ag_r.at[g],
                device_id=target, device_id_type=MESH).start()
            return inner
        lax.fori_loop(1, 16, one, 0)
        return carry

    lax.fori_loop(0, GROUPS, sum_z, 0)

    def agg_copy(c):
        return pltpu.make_async_copy(mombuf.at[c], agg_out.at[:, columns(c)], oa_sem.at[c])

    def new_weight_copy(c):
        return pltpu.make_async_copy(wbuf.at[c], weight_out.at[:, columns(c)], ow_sem.at[c])

    def expand_mean(g, carry):
        pltpu.make_async_copy(rsr.at[g, :, 0], rsr.at[g, :, 0], ag_r.at[g]).wait()
        for half in (0, 1):
            c = 2 * g + half
            load_weight(c).wait()
            for h in (0, 1):
                j = 2 * half + h
                wide = slice(256 * h, 256 * h + 256)
                agg = inverse(mask[g, j] * (mean[g, j] / 32.0))
                mombuf[c, :, wide] = agg
                wbuf[c, :, wide] = (wbuf[c, :, wide].astype(f32) - step_rate * agg).astype(jnp.bfloat16)
            agg_copy(c).start()
            new_weight_copy(c).start()
        return carry

    lax.fori_loop(0, GROUPS, expand_mean, 0)

    def moment_copy(c):
        return pltpu.make_async_copy(zrecv.at[c], moment_out.at[0, :, columns(c)], om_sem.at[c])

    def finish(g, carry):
        for half in (0, 1):
            c = 2 * g + half
            z_copy(c).wait_recv()
            for h in (0, 1):
                wide = slice(256 * h, 256 * h + 256)
                moment = sib[1, c, :, wide] + zrecv[c, :, wide]
                zrecv[c, :, wide] = moment - inverse(mask[g, 2 * half + h] * forward(moment))
            moment_copy(c).start()
        return carry

    lax.fori_loop(0, GROUPS, finish, 0)

    for c in range(CHUNKS - SLOTS, CHUNKS):
        for n in (0, 1):
            sib_copy(c, n).wait_send()

    def drain_chunk(c, carry):
        z_copy(c).wait_send()
        agg_copy(c).wait()
        new_weight_copy(c).wait()
        moment_copy(c).wait()
        return carry

    def drain_group(g, carry):
        pltpu.make_async_copy(rsr.at[g], rsr.at[g], rs_s.at[g]).wait()
        pltpu.make_async_copy(rsr.at[g, :, 0], rsr.at[g, :, 0], ag_s.at[g]).wait()
        for dz in (1, 2, 3):
            z3_copy(g, dz).wait_send()
        return carry

    lax.fori_loop(0, GROUPS, drain_group, 0)
    lax.fori_loop(0, CHUNKS, drain_chunk, 0)


def per_device(partials, momentum, weight, kept):
    left, right, left_t, right_t = (jnp.asarray(t) for t in low_tables())
    f32, bf16, i32 = jnp.float32, jnp.bfloat16, jnp.int32
    dma = pltpu.SemaphoreType.DMA
    vmem = pltpu.VMEM
    hbm = pl.BlockSpec(memory_space=pl.ANY)
    return pl.pallas_call(
        kernel,
        out_shape=(
            jax.ShapeDtypeStruct((1, ROWS, QUARTER), f32),
            jax.ShapeDtypeStruct((ROWS, QUARTER), f32),
            jax.ShapeDtypeStruct((ROWS, QUARTER), bf16),
        ),
        in_specs=[hbm] * 8,
        out_specs=(hbm,) * 3,
        scratch_shapes=[
            vmem((CHUNKS, 4, ROWS, CHUNK), bf16),
            vmem((SLOTS, 2, ROWS, CHUNK), f32),
            vmem((2, CHUNKS, ROWS, CHUNK), f32),
            vmem((CHUNKS, ROWS, CHUNK), f32),
            vmem((CHUNKS, ROWS, CHUNK), f32),
            vmem((CHUNKS, ROWS, CHUNK), bf16),
            vmem((GROUPS, 2, 4, LOW, 128), f32),
            vmem((GROUPS, 15, 2, PIECE, 128), f32),
            vmem((GROUPS, 2, PIECE, 128), f32),
            vmem((GROUPS, 3, PIECE, 128), f32),
            vmem((GROUPS, 4, LOW, 128), f32),
            vmem((GROUPS, 4, LOW, 128), f32),
            vmem((6, 224, 64), i32),
            vmem((6, 16, 224), i32),
            vmem((2, LOW, ROWS), bf16),
            vmem((2, 256, 128), bf16),
            vmem((2, ROWS, LOW), bf16),
            vmem((2, 128, 256), bf16),
            dma((5,)), dma((CHUNKS,)), dma((CHUNKS,)), dma((CHUNKS,)),
            dma((SLOTS, 2)), dma((CHUNKS, 2)), dma((CHUNKS,)), dma((CHUNKS,)),
            dma((GROUPS,)), dma((GROUPS,)), dma((GROUPS, 3)), dma((GROUPS, 3)), dma((GROUPS,)), dma((GROUPS,)),
            dma((CHUNKS,)), dma((CHUNKS,)), dma((CHUNKS,)),
        ],
        compiler_params=pltpu.CompilerParams(
            collective_id=0, has_side_effects=True, vmem_limit_bytes=56 * 2 ** 20),
        cost_estimate=pl.CostEstimate(flops=8 * 10 ** 9, bytes_accessed=34 * 10 ** 6, transcendentals=0),
        name="compress_step",
    )(partials, momentum, weight, kept, left, right, left_t, right_t)


def solution(mesh):
    placed = (
        P("rep", "shard", None, None),
        P("rep", None, "shard"),
        P(None, "shard"),
        P(None, "shard", None),
    )
    return jax.shard_map(
        per_device,
        mesh=mesh,
        in_specs=placed,
        out_specs=(P("rep", None, "shard"), P(None, "shard"), P(None, "shard")),
        check_vma=False,
    )
```

```python
import functools

import jax
import jax.numpy as jnp
import numpy as np
from jax import lax
from jax.experimental import pallas as pl
from jax.experimental.pallas import tpu as pltpu
from jax.sharding import PartitionSpec as P

decay_rate = 0.9
step_rate = 0.5

MESH = pl.DeviceIdType.MESH
ROWS = 192
LOW = 96
CHUNK = 512
CHUNKS = 14
GROUPS = 7
QUARTER = CHUNK * CHUNKS
SLOTS = 4
PIECE = 24
EARLY = 7


def low_tables():
    freq = np.arange(16, dtype=np.float64)[:, None]
    place = np.arange(32, dtype=np.float64)[None, :]
    low = np.cos(np.pi * (2.0 * place + 1.0) * freq / 64.0) * np.sqrt(2.0 / 32.0)
    low[0] *= np.sqrt(0.5)
    left = np.kron(np.eye(6), low)
    right = np.kron(np.eye(8), low.T)

    return tuple(np.ascontiguousarray(t, dtype=np.float32) for t in (left, right, left.T, right.T))


def split_dot(a, b):
    if isinstance(a, tuple):
        a_high, a_rest = a
        b_high = b.astype(jnp.bfloat16)
        b_rest = (b - b_high.astype(jnp.float32)).astype(jnp.bfloat16)
    else:
        b_high, b_rest = b
        a_high = a.astype(jnp.bfloat16)
        a_rest = (a - a_high.astype(jnp.float32)).astype(jnp.bfloat16)
    dot = functools.partial(jnp.dot, preferred_element_type=jnp.float32)
    return dot(a_high, b_high) + (dot(a_high, b_rest) + dot(a_rest, b_high))


def kernel(part, mom, wt, kept, left_in, right_in, left_t_in, right_t_in,
           moment_out, agg_out, weight_out,
           pbuf, stage, sib, zrecv, mombuf, wbuf, cf, rsr, red, z3r, mean, mask, keptb, rowbits,
           left32, right32, left_t32, right_t32, left, right, left_t, right_t,
           const_sem, p_sem, m_sem, w_sem, ss_sem, sr_sem, zs_sem, zr_sem,
           rs_s, rs_r, z3_s, z3_r, ag_s, ag_r, om_sem, oa_sem, ow_sem):
    f32 = jnp.float32
    rep, shard = lax.axis_index("rep"), lax.axis_index("shard")
    plane, z_hi = rep // 2, rep % 2
    y, x = plane // 4, plane % 4
    z_lo, core = shard // 2, shard % 2
    z = z_hi * 2 + z_lo

    def in_plane(k):
        py, px = (y + k // 4) % 4, (x + k % 4) % 4
        return py, px, ((py * 4 + px) * 2 + z_hi, shard)

    def along_z(dz):
        other = (z + dz) % 4
        return (plane * 2 + other // 2, (other % 2) * 2 + core)

    sibling = (rep, z_lo * 2 + (1 - core))
    partner = (rep, (1 - z_lo) * 2 + core)
    quarters = ((1 - z_lo) * 2 + (1 - core), z_lo * 2 + (1 - core), (1 - z_lo) * 2 + core, shard)

    def load_part(c):
        return [
            pltpu.make_async_copy(
                part.at[0, 0, :, pl.ds(pl.multiple_of(q * QUARTER + c * CHUNK, CHUNK), CHUNK)],
                pbuf.at[c, n], p_sem.at[c])
            for n, q in enumerate(quarters)
        ]

    def columns(c):
        return pl.ds(pl.multiple_of(c * CHUNK, CHUNK), CHUNK)

    def load_mom(c):
        return pltpu.make_async_copy(mom.at[0, :, columns(c)], mombuf.at[c], m_sem.at[c])

    def load_weight(c):
        return pltpu.make_async_copy(wt.at[:, columns(c)], wbuf.at[c], w_sem.at[c])

    consts = [
        pltpu.make_async_copy(src, dst, const_sem.at[n])
        for n, (src, dst) in enumerate(
            ((left_in, left32), (right_in, right32), (left_t_in, left_t32), (right_t_in, right_t32), (kept, keptb)))
    ]

    def start_part(c, carry):
        for copy in load_part(c):
            copy.start()
        return carry

    def start_rest(c, carry):
        load_mom(c).start()
        load_weight(c).start()
        return carry

    start_part(0, 0)
    for copy in consts:
        copy.start()
    lax.fori_loop(1, CHUNKS, start_part, 0)
    lax.fori_loop(0, CHUNKS, start_rest, 0)

    barrier = pltpu.get_barrier_semaphore()
    pl.semaphore_signal(barrier, inc=1, device_id=sibling, device_id_type=MESH)

    def greet(k, carry):
        pl.semaphore_signal(barrier, inc=1, device_id=in_plane(k)[2], device_id_type=MESH)
        return carry

    lax.fori_loop(1, 16, greet, 0)
    for dz in (1, 2, 3):
        pl.semaphore_signal(barrier, inc=1, device_id=along_z(dz), device_id_type=MESH)
    pl.semaphore_wait(barrier, 19)

    def forward(block):
        lefted = split_dot((left[0], left[1]), block)
        return split_dot(lefted, (right[0], right[1]))

    def inverse(low):
        wide = split_dot(low, (right_t[0], right_t[1]))
        return split_dot((left_t[0], left_t[1]), wide)

    def sib_copy(c, n):
        return pltpu.make_async_remote_copy(
            src_ref=stage.at[c % SLOTS, n], dst_ref=sib.at[n, c],
            send_sem=ss_sem.at[c % SLOTS, n], recv_sem=sr_sem.at[c, n],
            device_id=sibling, device_id_type=MESH)

    def z_copy(c):
        return pltpu.make_async_remote_copy(
            src_ref=sib.at[0, c], dst_ref=zrecv.at[c],
            send_sem=zs_sem.at[c], recv_sem=zr_sem.at[c],
            device_id=partner, device_id_type=MESH)

    def send_stage(c):
        pltpu.make_async_copy(pbuf.at[c], pbuf.at[c], p_sem.at[c]).wait()
        for n in (0, 1):
            @pl.when(c >= SLOTS)
            def _():
                sib_copy(c, n).wait_send()
            stage[c % SLOTS, n] = pbuf[c, n].astype(f32)
            sib_copy(c, n).start()

    def process(g, half):
        c = 2 * g + half
        sib_copy(c, 0).wait_recv()
        sib[0, c] = sib[0, c] + pbuf[c, 2].astype(f32)
        pl.when(c < EARLY)(lambda: z_copy(c).start())
        for h in (0, 1):
            cf[g, 1, 2 * half + h] = forward(sib[0, c, :, 256 * h:256 * h + 256])
        sib_copy(c, 1).wait_recv()
        load_mom(c).wait()
        sib[1, c] = sib[1, c] + pbuf[c, 3].astype(f32) + decay_rate * mombuf[c]
        for h in (0, 1):
            cf[g, 0, 2 * half + h] = forward(sib[1, c, :, 256 * h:256 * h + 256])

    def rs_send(g):
        def one(k, carry):
            py, px, target = in_plane(k)
            pltpu.make_async_remote_copy(
                src_ref=cf.at[g, :, py, pl.ds(pl.multiple_of(px * PIECE, 8), PIECE)],
                dst_ref=rsr.at[g, k - 1],
                send_sem=rs_s.at[g], recv_sem=rs_r.at[g],
                device_id=target, device_id_type=MESH).start()
            return carry
        lax.fori_loop(1, 16, one, 0)

    send_stage(0)
    for copy in consts:
        copy.wait()
    for whole, pair in ((left32, left), (right32, right), (left_t32, left_t), (right_t32, right_t)):
        high = whole[...].astype(jnp.bfloat16)
        pair[0] = high
        pair[1] = (whole[...] - high.astype(f32)).astype(jnp.bfloat16)

    def gather_chip(g, carry):
        send_stage(2 * g + 1)
        process(g, 0)

        @pl.when(g < GROUPS - 1)
        def _():
            send_stage(2 * g + 2)
        process(g, 1)
        rs_send(g)
        return carry

    lax.fori_loop(0, GROUPS, gather_chip, 0)

    def band_words(b, carry):
        at = keptb[b]
        row, word = at // 32, jnp.left_shift(jnp.ones_like(at), at % 32)
        for k in range(16):
            rowbits[b, pl.ds(k, 1), :] = jnp.sum(jnp.where(row == k, word, 0), axis=0, keepdims=True)
        return carry

    lax.fori_loop(0, 6, band_words, 0)

    def group_mask(g, carry):
        words = rowbits[...].reshape(LOW, 224)
        upper = (words // 256).astype(f32).astype(jnp.bfloat16)
        lower = (words % 256).astype(f32).astype(jnp.bfloat16)
        block = lax.broadcasted_iota(jnp.int32, (224, 128), 0)
        lane = lax.broadcasted_iota(jnp.int32, (224, 128), 1)
        bit = lax.broadcasted_iota(jnp.int32, (LOW, 128), 1) % 16
        for j in range(4):
            spread = (block == (g * 4 + j) * 8 + lane // 16).astype(f32).astype(jnp.bfloat16)
            high = jnp.dot(upper, spread, preferred_element_type=f32)
            low = jnp.dot(lower, spread, preferred_element_type=f32)
            word = (high * 256.0 + low).astype(jnp.int32)
            mask[g, j] = (jnp.right_shift(word, bit) & 1).astype(f32)
        return carry

    lax.fori_loop(0, GROUPS, group_mask, 0)

    mine = pl.ds(pl.multiple_of(x * PIECE, 8), PIECE)

    def z3_copy(g, dz):
        return pltpu.make_async_remote_copy(
            src_ref=red.at[g, dz % 2], dst_ref=z3r.at[g, dz - 1],
            send_sem=z3_s.at[g, dz - 1], recv_sem=z3_r.at[g, dz - 1],
            device_id=along_z(dz), device_id_type=MESH)

    def sum_plane(g, carry):
        pltpu.make_async_copy(rsr.at[g], rsr.at[g], rs_r.at[g]).wait()
        for n in (0, 1):
            total = cf[g, n, y, mine]
            for k in range(15):
                total = total + rsr[g, k, n]
            red[g, n] = total
        for dz in (1, 2, 3):
            z3_copy(g, dz).start()
        return carry

    lax.fori_loop(0, GROUPS, sum_plane, 0)

    def start_z(c, carry):
        z_copy(c).start()
        return carry

    lax.fori_loop(EARLY, CHUNKS, start_z, 0)

    def sum_z(g, carry):
        for dz in (1, 2, 3):
            z3_copy(g, dz).wait_recv()
        mean[g, y, mine] = red[g, 0] + (z3r[g, 0] + z3r[g, 1] + z3r[g, 2])

        def one(k, inner):
            target = in_plane(k)[2]
            pltpu.make_async_remote_copy(
                src_ref=mean.at[g, y, mine], dst_ref=mean.at[g, y, mine],
                send_sem=ag_s.at[g], recv_sem=ag_r.at[g],
                device_id=target, device_id_type=MESH).start()
            return inner
        lax.fori_loop(1, 16, one, 0)
        return carry

    lax.fori_loop(0, GROUPS, sum_z, 0)

    def agg_copy(c):
        return pltpu.make_async_copy(mombuf.at[c], agg_out.at[:, columns(c)], oa_sem.at[c])

    def new_weight_copy(c):
        return pltpu.make_async_copy(wbuf.at[c], weight_out.at[:, columns(c)], ow_sem.at[c])

    def expand_mean(g, carry):
        pltpu.make_async_copy(rsr.at[g, :, 0], rsr.at[g, :, 0], ag_r.at[g]).wait()
        for half in (0, 1):
            c = 2 * g + half
            load_weight(c).wait()
            for h in (0, 1):
                j = 2 * half + h
                wide = slice(256 * h, 256 * h + 256)
                agg = inverse(mask[g, j] * (mean[g, j] / 32.0))
                mombuf[c, :, wide] = agg
                wbuf[c, :, wide] = (wbuf[c, :, wide].astype(f32) - step_rate * agg).astype(jnp.bfloat16)
            agg_copy(c).start()
            new_weight_copy(c).start()
        return carry

    lax.fori_loop(0, GROUPS, expand_mean, 0)

    def moment_copy(c):
        return pltpu.make_async_copy(zrecv.at[c], moment_out.at[0, :, columns(c)], om_sem.at[c])

    def finish(g, carry):
        for half in (0, 1):
            c = 2 * g + half
            z_copy(c).wait_recv()
            for h in (0, 1):
                wide = slice(256 * h, 256 * h + 256)
                moment = sib[1, c, :, wide] + zrecv[c, :, wide]
                zrecv[c, :, wide] = moment - inverse(mask[g, 2 * half + h] * forward(moment))
            moment_copy(c).start()
        return carry

    lax.fori_loop(0, GROUPS, finish, 0)

    for c in range(CHUNKS - SLOTS, CHUNKS):
        for n in (0, 1):
            sib_copy(c, n).wait_send()

    def drain_chunk(c, carry):
        z_copy(c).wait_send()
        agg_copy(c).wait()
        new_weight_copy(c).wait()
        moment_copy(c).wait()
        return carry

    def drain_group(g, carry):
        pltpu.make_async_copy(rsr.at[g], rsr.at[g], rs_s.at[g]).wait()
        pltpu.make_async_copy(rsr.at[g, :, 0], rsr.at[g, :, 0], ag_s.at[g]).wait()
        for dz in (1, 2, 3):
            z3_copy(g, dz).wait_send()
        return carry

    lax.fori_loop(0, GROUPS, drain_group, 0)
    lax.fori_loop(0, CHUNKS, drain_chunk, 0)


def per_device(partials, momentum, weight, kept):
    left, right, left_t, right_t = (jnp.asarray(t) for t in low_tables())
    f32, bf16, i32 = jnp.float32, jnp.bfloat16, jnp.int32
    dma = pltpu.SemaphoreType.DMA
    vmem = pltpu.VMEM
    hbm = pl.BlockSpec(memory_space=pl.ANY)
    return pl.pallas_call(
        kernel,
        out_shape=(
            jax.ShapeDtypeStruct((1, ROWS, QUARTER), f32),
            jax.ShapeDtypeStruct((ROWS, QUARTER), f32),
            jax.ShapeDtypeStruct((ROWS, QUARTER), bf16),
        ),
        in_specs=[hbm] * 8,
        out_specs=(hbm,) * 3,
        scratch_shapes=[
            vmem((CHUNKS, 4, ROWS, CHUNK), bf16),
            vmem((SLOTS, 2, ROWS, CHUNK), f32),
            vmem((2, CHUNKS, ROWS, CHUNK), f32),
            vmem((CHUNKS, ROWS, CHUNK), f32),
            vmem((CHUNKS, ROWS, CHUNK), f32),
            vmem((CHUNKS, ROWS, CHUNK), bf16),
            vmem((GROUPS, 2, 4, LOW, 128), f32),
            vmem((GROUPS, 15, 2, PIECE, 128), f32),
            vmem((GROUPS, 2, PIECE, 128), f32),
            vmem((GROUPS, 3, PIECE, 128), f32),
            vmem((GROUPS, 4, LOW, 128), f32),
            vmem((GROUPS, 4, LOW, 128), f32),
            vmem((6, 64, 224), i32),
            vmem((6, 16, 224), i32),
            vmem((LOW, ROWS), f32),
            vmem((256, 128), f32),
            vmem((ROWS, LOW), f32),
            vmem((128, 256), f32),
            vmem((2, LOW, ROWS), bf16),
            vmem((2, 256, 128), bf16),
            vmem((2, ROWS, LOW), bf16),
            vmem((2, 128, 256), bf16),
            dma((5,)), dma((CHUNKS,)), dma((CHUNKS,)), dma((CHUNKS,)),
            dma((SLOTS, 2)), dma((CHUNKS, 2)), dma((CHUNKS,)), dma((CHUNKS,)),
            dma((GROUPS,)), dma((GROUPS,)), dma((GROUPS, 3)), dma((GROUPS, 3)), dma((GROUPS,)), dma((GROUPS,)),
            dma((CHUNKS,)), dma((CHUNKS,)), dma((CHUNKS,)),
        ],
        compiler_params=pltpu.CompilerParams(
            collective_id=0, has_side_effects=True, vmem_limit_bytes=56 * 2 ** 20),
        cost_estimate=pl.CostEstimate(flops=8 * 10 ** 9, bytes_accessed=34 * 10 ** 6, transcendentals=0),
        name="compress_step",
    )(partials, momentum, weight, jnp.transpose(kept, (0, 2, 1)), left, right, left_t, right_t)


def solution(mesh):
    placed = (
        P("rep", "shard", None, None),
        P("rep", None, "shard"),
        P(None, "shard"),
        P(None, "shard", None),
    )
    return jax.shard_map(
        per_device,
        mesh=mesh,
        in_specs=placed,
        out_specs=(P("rep", None, "shard"), P(None, "shard"), P(None, "shard")),
        check_vma=False,
    )
```

```python
import functools

import jax
import jax.numpy as jnp
import numpy as np
from jax import lax
from jax.experimental import pallas as pl
from jax.experimental.pallas import tpu as pltpu
from jax.sharding import PartitionSpec as P

decay_rate = 0.9
step_rate = 0.5

MESH = pl.DeviceIdType.MESH
ROWS = 192
LOW = 96
CHUNK = 512
CHUNKS = 14
GROUPS = 7
QUARTER = CHUNK * CHUNKS
SLOTS = 4
LOADS = 8
PIECE = 24
EARLY = 7


def low_tables():
    freq = np.arange(16, dtype=np.float64)[:, None]
    place = np.arange(32, dtype=np.float64)[None, :]
    low = np.cos(np.pi * (2.0 * place + 1.0) * freq / 64.0) * np.sqrt(2.0 / 32.0)
    low[0] *= np.sqrt(0.5)
    left = np.kron(np.eye(6), low)
    right = np.kron(np.eye(8), low.T)

    return tuple(np.ascontiguousarray(t, dtype=np.float32) for t in (left, right, left.T, right.T))


def split_dot(a, b):
    if isinstance(a, tuple):
        a_high, a_rest = a
        b_high = b.astype(jnp.bfloat16)
        b_rest = (b - b_high.astype(jnp.float32)).astype(jnp.bfloat16)
    else:
        b_high, b_rest = b
        a_high = a.astype(jnp.bfloat16)
        a_rest = (a - a_high.astype(jnp.float32)).astype(jnp.bfloat16)
    dot = functools.partial(jnp.dot, preferred_element_type=jnp.float32)
    return dot(a_high, b_high) + (dot(a_high, b_rest) + dot(a_rest, b_high))


def kernel(part, mom, wt, kept, left_in, right_in, left_t_in, right_t_in,
           moment_out, agg_out, weight_out,
           pbuf, stage, sib, zrecv, mombuf, wbuf, cf, rsr, red, z3r, mean, mask, keptb, rowbits,
           left32, right32, left_t32, right_t32, left, right, left_t, right_t,
           const_sem, p_sem, m_sem, w_sem, ss_sem, sr_sem, zs_sem, zr_sem,
           rs_s, rs_r, z3_s, z3_r, ag_s, ag_r, om_sem, oa_sem, ow_sem, ready_sem, plane_sem):
    f32 = jnp.float32
    rep, shard = lax.axis_index("rep"), lax.axis_index("shard")
    plane, z_hi = rep // 2, rep % 2
    y, x = plane // 4, plane % 4
    z_lo, core = shard // 2, shard % 2
    z = z_hi * 2 + z_lo

    def in_plane(k):
        py, px = (y + k // 4) % 4, (x + k % 4) % 4
        return py, px, ((py * 4 + px) * 2 + z_hi, shard)

    def along_z(dz):
        other = (z + dz) % 4
        return (plane * 2 + other // 2, (other % 2) * 2 + core)

    sibling = (rep, z_lo * 2 + (1 - core))
    partner = (rep, (1 - z_lo) * 2 + core)
    quarters = ((1 - z_lo) * 2 + (1 - core), z_lo * 2 + (1 - core), (1 - z_lo) * 2 + core, shard)

    def load_part(c):
        return [
            pltpu.make_async_copy(
                part.at[0, 0, :, pl.ds(pl.multiple_of(q * QUARTER + c * CHUNK, CHUNK), CHUNK)],
                pbuf.at[c % LOADS, n], p_sem.at[c % LOADS])
            for n, q in enumerate(quarters)
        ]

    def columns(c):
        return pl.ds(pl.multiple_of(c * CHUNK, CHUNK), CHUNK)

    def load_mom(c):
        return pltpu.make_async_copy(mom.at[0, :, columns(c)], mombuf.at[c], m_sem.at[c])

    def load_weight(c):
        return pltpu.make_async_copy(wt.at[:, columns(c)], wbuf.at[c], w_sem.at[c])

    consts = [
        pltpu.make_async_copy(src, dst, const_sem.at[n])
        for n, (src, dst) in enumerate(
            ((left_in, left32), (right_in, right32), (left_t_in, left_t32), (right_t_in, right_t32), (kept, keptb)))
    ]

    def start_part(c, carry):
        for copy in load_part(c):
            copy.start()
        return carry

    def start_rest(c, carry):
        load_mom(c).start()
        load_weight(c).start()
        return carry

    barrier = pltpu.get_barrier_semaphore()
    leads = z_lo == core

    @pl.when(jnp.logical_not(leads))
    def _():
        for other in (sibling, partner):
            pl.semaphore_signal(barrier, inc=1, device_id=other, device_id_type=MESH)

    start_part(0, 0)

    @pl.when(leads)
    def _():
        pl.semaphore_wait(barrier, 2)
        for other in (sibling, partner):
            pl.semaphore_signal(ready_sem, inc=1, device_id=other, device_id_type=MESH)

    @pl.when(jnp.logical_not(leads))
    def _():
        pl.semaphore_wait(ready_sem, 2)

        def greet(k, carry):
            pl.semaphore_signal(barrier, inc=1, device_id=in_plane(k)[2], device_id_type=MESH)
            return carry

        lax.fori_loop(1, 16, greet, 0)
        pl.semaphore_signal(barrier, inc=1, device_id=along_z(2), device_id_type=MESH)

    def meet_plane():
        @pl.when(jnp.logical_not(leads))
        def _():
            pl.semaphore_wait(barrier, 16)
            pl.semaphore_signal(plane_sem, inc=1, device_id=sibling, device_id_type=MESH)

        @pl.when(leads)
        def _():
            pl.semaphore_wait(plane_sem, 1)

    def forward(block):
        lefted = split_dot((left[0], left[1]), block)
        return split_dot(lefted, (right[0], right[1]))

    def inverse(low):
        wide = split_dot(low, (right_t[0], right_t[1]))
        return split_dot((left_t[0], left_t[1]), wide)

    def sib_copy(c, n):
        return pltpu.make_async_remote_copy(
            src_ref=stage.at[c % SLOTS, n], dst_ref=sib.at[n, c],
            send_sem=ss_sem.at[c % SLOTS, n], recv_sem=sr_sem.at[c, n],
            device_id=sibling, device_id_type=MESH)

    def z_copy(c):
        return pltpu.make_async_remote_copy(
            src_ref=sib.at[0, c], dst_ref=zrecv.at[c],
            send_sem=zs_sem.at[c], recv_sem=zr_sem.at[c],
            device_id=partner, device_id_type=MESH)

    def send_stage(c):
        pltpu.make_async_copy(pbuf.at[c % LOADS], pbuf.at[c % LOADS], p_sem.at[c % LOADS]).wait()
        for n in (0, 1):
            @pl.when(c >= SLOTS)
            def _():
                sib_copy(c, n).wait_send()
            stage[c % SLOTS, n] = pbuf[c % LOADS, n].astype(f32)
            sib_copy(c, n).start()

    def process(g, half):
        c = 2 * g + half
        sib_copy(c, 0).wait_recv()
        sib[0, c] = sib[0, c] + pbuf[c % LOADS, 2].astype(f32)
        pl.when(c < EARLY)(lambda: z_copy(c).start())
        for h in (0, 1):
            cf[g, 1, 2 * half + h] = forward(sib[0, c, :, 256 * h:256 * h + 256])
        sib_copy(c, 1).wait_recv()
        load_mom(c).wait()
        sib[1, c] = sib[1, c] + pbuf[c % LOADS, 3].astype(f32) + decay_rate * mombuf[c]
        pl.when(c + LOADS < CHUNKS)(lambda: start_part(c + LOADS, None))
        for h in (0, 1):
            cf[g, 0, 2 * half + h] = forward(sib[1, c, :, 256 * h:256 * h + 256])

    def rs_send(g):
        def one(k, carry):
            py, px, target = in_plane(k)
            pltpu.make_async_remote_copy(
                src_ref=cf.at[g, :, py, pl.ds(pl.multiple_of(px * PIECE, 8), PIECE)],
                dst_ref=rsr.at[g, k - 1],
                send_sem=rs_s.at[g], recv_sem=rs_r.at[g],
                device_id=target, device_id_type=MESH).start()
            return carry
        lax.fori_loop(1, 16, one, 0)

    send_stage(0)
    for copy in consts:
        copy.start()
    lax.fori_loop(1, LOADS, start_part, 0)
    lax.fori_loop(0, CHUNKS, start_rest, 0)
    for copy in consts:
        copy.wait()
    for whole, pair in ((left32, left), (right32, right), (left_t32, left_t), (right_t32, right_t)):
        high = whole[...].astype(jnp.bfloat16)
        pair[0] = high
        pair[1] = (whole[...] - high.astype(f32)).astype(jnp.bfloat16)

    def gather_chip(g, carry):
        send_stage(2 * g + 1)
        process(g, 0)

        @pl.when(g < GROUPS - 1)
        def _():
            send_stage(2 * g + 2)
        process(g, 1)
        pl.when(g == 0)(meet_plane)
        rs_send(g)
        return carry

    lax.fori_loop(0, GROUPS, gather_chip, 0)

    def band_words(b, carry):
        at = keptb[b]
        row, word = at // 32, jnp.left_shift(jnp.ones_like(at), at % 32)
        for k in range(16):
            rowbits[b, pl.ds(k, 1), :] = jnp.sum(jnp.where(row == k, word, 0), axis=0, keepdims=True)
        return carry

    lax.fori_loop(0, 6, band_words, 0)

    def group_mask(g, carry):
        words = rowbits[...].reshape(LOW, 224)
        upper = (words // 256).astype(f32).astype(jnp.bfloat16)
        lower = (words % 256).astype(f32).astype(jnp.bfloat16)
        block = lax.broadcasted_iota(jnp.int32, (224, 128), 0)
        lane = lax.broadcasted_iota(jnp.int32, (224, 128), 1)
        bit = lax.broadcasted_iota(jnp.int32, (LOW, 128), 1) % 16
        for j in range(4):
            spread = (block == (g * 4 + j) * 8 + lane // 16).astype(f32).astype(jnp.bfloat16)
            high = jnp.dot(upper, spread, preferred_element_type=f32)
            low = jnp.dot(lower, spread, preferred_element_type=f32)
            word = (high * 256.0 + low).astype(jnp.int32)
            mask[g, j] = (jnp.right_shift(word, bit) & 1).astype(f32)
        return carry

    lax.fori_loop(0, GROUPS, group_mask, 0)

    mine = pl.ds(pl.multiple_of(x * PIECE, 8), PIECE)

    def z3_copy(g, step):
        target = along_z(jnp.where(z_lo == 1, 1, 3)) if step == 0 else along_z(2)
        return pltpu.make_async_remote_copy(
            src_ref=red.at[g, 1 - step], dst_ref=z3r.at[g, step],
            send_sem=z3_s.at[g, step], recv_sem=z3_r.at[g, step],
            device_id=target, device_id_type=MESH)

    def sum_plane(g, carry):
        pltpu.make_async_copy(rsr.at[g], rsr.at[g], rs_r.at[g]).wait()
        for n in (0, 1):
            total = cf[g, n, y, mine]
            for k in range(15):
                total = total + rsr[g, k, n]
            red[g, n] = total
        z3_copy(g, 0).start()
        return carry

    lax.fori_loop(0, GROUPS, sum_plane, 0)

    def sum_pair(g, carry):
        z3_copy(g, 0).wait_recv()
        red[g, 0] = red[g, 0] + z3r[g, 0]
        z3_copy(g, 1).start()
        return carry

    lax.fori_loop(0, GROUPS, sum_pair, 0)

    def start_z(c, carry):
        z_copy(c).start()
        return carry

    lax.fori_loop(EARLY, CHUNKS, start_z, 0)

    def sum_z(g, carry):
        z3_copy(g, 1).wait_recv()
        mean[g, y, mine] = red[g, 0] + z3r[g, 1]

        def one(k, inner):
            target = in_plane(k)[2]
            pltpu.make_async_remote_copy(
                src_ref=mean.at[g, y, mine], dst_ref=mean.at[g, y, mine],
                send_sem=ag_s.at[g], recv_sem=ag_r.at[g],
                device_id=target, device_id_type=MESH).start()
            return inner
        lax.fori_loop(1, 16, one, 0)
        return carry

    lax.fori_loop(0, GROUPS, sum_z, 0)

    def agg_copy(c):
        return pltpu.make_async_copy(mombuf.at[c], agg_out.at[:, columns(c)], oa_sem.at[c])

    def new_weight_copy(c):
        return pltpu.make_async_copy(wbuf.at[c], weight_out.at[:, columns(c)], ow_sem.at[c])

    def expand_mean(g, carry):
        pltpu.make_async_copy(rsr.at[g, :, 0], rsr.at[g, :, 0], ag_r.at[g]).wait()
        for half in (0, 1):
            c = 2 * g + half
            load_weight(c).wait()
            for h in (0, 1):
                j = 2 * half + h
                wide = slice(256 * h, 256 * h + 256)
                agg = inverse(mask[g, j] * (mean[g, j] / 32.0))
                mombuf[c, :, wide] = agg
                wbuf[c, :, wide] = (wbuf[c, :, wide].astype(f32) - step_rate * agg).astype(jnp.bfloat16)
            agg_copy(c).start()
            new_weight_copy(c).start()
        return carry

    lax.fori_loop(0, GROUPS, expand_mean, 0)

    def moment_copy(c):
        return pltpu.make_async_copy(zrecv.at[c], moment_out.at[0, :, columns(c)], om_sem.at[c])

    def finish(g, carry):
        for half in (0, 1):
            c = 2 * g + half
            z_copy(c).wait_recv()
            for h in (0, 1):
                wide = slice(256 * h, 256 * h + 256)
                moment = sib[1, c, :, wide] + zrecv[c, :, wide]
                zrecv[c, :, wide] = moment - inverse(mask[g, 2 * half + h] * forward(moment))
            moment_copy(c).start()
        return carry

    lax.fori_loop(0, GROUPS, finish, 0)

    for c in range(CHUNKS - SLOTS, CHUNKS):
        for n in (0, 1):
            sib_copy(c, n).wait_send()

    def drain_chunk(c, carry):
        z_copy(c).wait_send()
        agg_copy(c).wait()
        new_weight_copy(c).wait()
        moment_copy(c).wait()
        return carry

    def drain_group(g, carry):
        pltpu.make_async_copy(rsr.at[g], rsr.at[g], rs_s.at[g]).wait()
        pltpu.make_async_copy(rsr.at[g, :, 0], rsr.at[g, :, 0], ag_s.at[g]).wait()
        for step in (0, 1):
            z3_copy(g, step).wait_send()
        return carry

    lax.fori_loop(0, GROUPS, drain_group, 0)
    lax.fori_loop(0, CHUNKS, drain_chunk, 0)


def write_out(*refs):
    ins, outs, sem = refs[:3], refs[3:6], refs[6]
    copies = []
    for n, (src, dst) in enumerate(zip(ins, outs)):
        if n == 0:
            src, dst = src.at[0], dst.at[0]
        for b in range(6):
            rows = pl.ds(32 * b, 32)
            copies.append(pltpu.make_async_copy(src.at[rows], dst.at[rows], sem.at[b, n]))
    for copy in copies:
        copy.start()
    for copy in copies:
        copy.wait()


def per_device(partials, momentum, weight, kept):
    left, right, left_t, right_t = (jnp.asarray(t) for t in low_tables())
    f32, bf16, i32 = jnp.float32, jnp.bfloat16, jnp.int32
    dma = pltpu.SemaphoreType.DMA
    vmem = pltpu.VMEM
    hbm = pl.BlockSpec(memory_space=pl.ANY)
    results = pl.pallas_call(
        kernel,
        out_shape=(
            vmem((1, ROWS, QUARTER), f32),
            vmem((ROWS, QUARTER), f32),
            vmem((ROWS, QUARTER), bf16),
        ),
        in_specs=[hbm] * 8,
        out_specs=(hbm,) * 3,
        scratch_shapes=[
            vmem((LOADS, 4, ROWS, CHUNK), bf16),
            vmem((SLOTS, 2, ROWS, CHUNK), f32),
            vmem((2, CHUNKS, ROWS, CHUNK), f32),
            vmem((CHUNKS, ROWS, CHUNK), f32),
            vmem((CHUNKS, ROWS, CHUNK), f32),
            vmem((CHUNKS, ROWS, CHUNK), bf16),
            vmem((GROUPS, 2, 4, LOW, 128), f32),
            vmem((GROUPS, 15, 2, PIECE, 128), f32),
            vmem((GROUPS, 2, PIECE, 128), f32),
            vmem((GROUPS, 2, PIECE, 128), f32),
            vmem((GROUPS, 4, LOW, 128), f32),
            vmem((GROUPS, 4, LOW, 128), f32),
            vmem((6, 64, 224), i32),
            vmem((6, 16, 224), i32),
            vmem((LOW, ROWS), f32),
            vmem((256, 128), f32),
            vmem((ROWS, LOW), f32),
            vmem((128, 256), f32),
            vmem((2, LOW, ROWS), bf16),
            vmem((2, 256, 128), bf16),
            vmem((2, ROWS, LOW), bf16),
            vmem((2, 128, 256), bf16),
            dma((5,)), dma((LOADS,)), dma((CHUNKS,)), dma((CHUNKS,)),
            dma((SLOTS, 2)), dma((CHUNKS, 2)), dma((CHUNKS,)), dma((CHUNKS,)),
            dma((GROUPS,)), dma((GROUPS,)), dma((GROUPS, 2)), dma((GROUPS, 2)), dma((GROUPS,)), dma((GROUPS,)),
            dma((CHUNKS,)), dma((CHUNKS,)), dma((CHUNKS,)),
            pltpu.SemaphoreType.REGULAR, pltpu.SemaphoreType.REGULAR,
        ],
        compiler_params=pltpu.CompilerParams(
            collective_id=0, has_side_effects=True, vmem_limit_bytes=46 * 2 ** 20),
        cost_estimate=pl.CostEstimate(flops=8 * 10 ** 9, bytes_accessed=34 * 10 ** 6, transcendentals=0),
        name="compress_step",
    )(partials, momentum, weight, jnp.transpose(kept, (0, 2, 1)), left, right, left_t, right_t)
    return pl.pallas_call(
        write_out,
        out_shape=tuple(jax.ShapeDtypeStruct(r.shape, r.dtype) for r in results),
        in_specs=[hbm] * 3,
        out_specs=(hbm,) * 3,
        scratch_shapes=[dma((6, 3))],
        compiler_params=pltpu.CompilerParams(vmem_limit_bytes=2 ** 20),
        name="write_out",
    )(*(pltpu.with_memory_space_constraint(r, vmem) for r in results))


def solution(mesh):
    placed = (
        P("rep", "shard", None, None),
        P("rep", None, "shard"),
        P(None, "shard"),
        P(None, "shard", None),
    )
    return jax.shard_map(
        per_device,
        mesh=mesh,
        in_specs=placed,
        out_specs=(P("rep", None, "shard"), P(None, "shard"), P(None, "shard")),
        check_vma=False,
    )
```

```python
import functools

import jax
import jax.numpy as jnp
import numpy as np
from jax import lax
from jax.experimental import pallas as pl
from jax.experimental.pallas import tpu as pltpu
from jax.sharding import PartitionSpec as P

decay_rate = 0.9
step_rate = 0.5

MESH = pl.DeviceIdType.MESH
ROWS = 192
LOW = 96
CHUNK = 256
CHUNKS = 28
GROUPS = 7
QUARTER = CHUNK * CHUNKS
SLOTS = 8
LOADS = 16
PIECE = 24
MOVES = 4
AHEAD = 3
MIDDLE = 4
RAW = 2
HALF = 2 * ROWS
PACKED = 360
EARLY = 20


def tables():
    freq = np.arange(32, dtype=np.float64)[:, None]
    place = np.arange(32, dtype=np.float64)[None, :]
    dct = np.cos(np.pi * (2.0 * place + 1.0) * freq / 64.0) * np.sqrt(2.0 / 32.0)
    dct[0] *= np.sqrt(0.5)
    left = np.zeros((ROWS, ROWS))
    for band in range(6):
        for k in range(16):
            left[32 * (band // 2) + 2 * k + band % 2, 32 * band:32 * band + 32] = dct[k]
            left[LOW + 16 * band + k, 32 * band:32 * band + 32] = dct[16 + k]
    right = np.concatenate([np.kron(np.eye(8), dct[:16].T), np.kron(np.eye(8), dct[16:].T)], axis=1)
    return tuple(np.ascontiguousarray(t, dtype=np.float32) for t in (left, right, left.T, right.T))


def two_terms(v):
    high = v.astype(jnp.bfloat16)
    return high, (v - high.astype(jnp.float32)).astype(jnp.bfloat16)


def split_dot(a, b):
    a_high, a_rest = a if isinstance(a, tuple) else two_terms(a)
    b_high, b_rest = b if isinstance(b, tuple) else two_terms(b)
    rows = a_high.shape[0]
    dot = functools.partial(jnp.dot, preferred_element_type=jnp.float32)
    first = dot(jnp.concatenate([a_high, a_rest], axis=0), b_high)
    return first[:rows] + (first[rows:] + dot(a_high, b_rest))


def kernel(part, mom, wt, kept, left_in, right_in, left_t_in, right_t_in,
           moment_out, agg_out, weight_out,
           pbuf, stage, stage_far, own, far, zrecv, mombuf, wbuf, cf, rsr, red, z3r, mean, mask, keptb, rowbits,
           kept_far, words_far, gives_of, same, before, above,
           left32, right32, left_t32, right_t32, left, right, left_t, right_t,
           const_sem, p_sem, m_sem, w_sem, ss_sem, sr_sem, zs_sem, zr_sem,
           rs_s, rs_r, z3_s, z3_r, ag_s, ag_r, om_sem, oa_sem, ow_sem, k_sem, ready_sem, plane_sem):
    f32 = jnp.float32
    rep, shard = lax.axis_index("rep"), lax.axis_index("shard")
    plane, z_hi = rep // 2, rep % 2
    y, x = plane // 4, plane % 4
    z_lo, core = shard // 2, shard % 2
    z = z_hi * 2 + z_lo

    def in_plane(k):
        py, px = (y + k // 4) % 4, (x + k % 4) % 4
        return py, px, ((py * 4 + px) * 2 + z_hi, shard)

    def along_z(dz):
        other = (z + dz) % 4
        return (plane * 2 + other // 2, (other % 2) * 2 + core)

    sibling = (rep, z_lo * 2 + (1 - core))
    partner = (rep, (1 - z_lo) * 2 + core)
    quarters = ((1 - z_lo) * 2 + (1 - core), z_lo * 2 + (1 - core), (1 - z_lo) * 2 + core, shard)

    def load_part(c):
        return [
            pltpu.make_async_copy(
                part.at[0, 0, :, pl.ds(pl.multiple_of(q * QUARTER + c * CHUNK, CHUNK), CHUNK)],
                pbuf.at[c % LOADS, n], p_sem.at[c % LOADS])
            for n, q in enumerate(quarters)
        ]

    def columns(c):
        return pl.ds(pl.multiple_of(c * CHUNK, CHUNK), CHUNK)

    def load_mom(c):
        return pltpu.make_async_copy(mom.at[0, :, columns(c)], mombuf.at[c], m_sem.at[c])

    def load_weight(c):
        return pltpu.make_async_copy(wt.at[:, columns(c)], wbuf.at[c], w_sem.at[c])

    consts = [
        pltpu.make_async_copy(src, dst, const_sem.at[n])
        for n, (src, dst) in enumerate(
            ((left_in, left32), (right_in, right32), (left_t_in, left_t32), (right_t_in, right_t32), (kept, keptb)))
    ]

    def start_part(c, carry):
        for copy in load_part(c):
            copy.start()
        return carry

    def start_rest(c, carry):
        load_mom(c).start()
        load_weight(c).start()
        return carry

    barrier = pltpu.get_barrier_semaphore()
    leads = z_lo == core

    @pl.when(jnp.logical_not(leads))
    def _():
        for other in (sibling, partner):
            pl.semaphore_signal(barrier, inc=1, device_id=other, device_id_type=MESH)

    start_part(0, 0)

    @pl.when(leads)
    def _():
        pl.semaphore_wait(barrier, 2)
        for other in (sibling, partner):
            pl.semaphore_signal(ready_sem, inc=1, device_id=other, device_id_type=MESH)

    @pl.when(jnp.logical_not(leads))
    def _():
        pl.semaphore_wait(ready_sem, 2)

        def greet(k, carry):
            pl.semaphore_signal(barrier, inc=1, device_id=in_plane(k)[2], device_id_type=MESH)
            return carry

        lax.fori_loop(1, 16, greet, 0)
        pl.semaphore_signal(barrier, inc=1, device_id=along_z(2), device_id_type=MESH)

    def meet_plane():
        @pl.when(jnp.logical_not(leads))
        def _():
            pl.semaphore_wait(barrier, 16)
            pl.semaphore_signal(plane_sem, inc=1, device_id=sibling, device_id_type=MESH)

        @pl.when(leads)
        def _():
            pl.semaphore_wait(plane_sem, 1)

    def forward(block):
        lefted = split_dot((left[0, :LOW], left[1, :LOW]), block)
        return split_dot(lefted, (right[0, :, :128], right[1, :, :128]))

    def inverse(low):
        wide = split_dot(low, (right_t[0, :128], right_t[1, :128]))
        return split_dot((left_t[0, :, :LOW], left_t[1, :, :LOW]), wide)

    row = lax.broadcasted_iota(jnp.int32, (LOW, 128), 0) % 32 // 2
    lane = lax.broadcasted_iota(jnp.int32, (LOW, 128), 1) % 16

    def turn(v, shift, axis):
        return pltpu.roll(v, shift % v.shape[axis], axis)

    def from_later(v, step):
        if step >= 4:
            return turn(v, -(2 << (step - 4)), 0)
        far = 1 << step
        return jnp.where(lane + far < 16, turn(v, -far, 1), turn(turn(v, -2, 0), 16 - far, 1))

    def from_earlier(v, step):
        if step >= 4:
            return turn(v, 2 << (step - 4), 0)
        far = 1 << step
        return jnp.where(lane >= far, turn(v, far, 1), turn(turn(v, 2, 0), -(16 - far), 1))

    def unpack_words(words, at):
        def band_words(p, carry):
            for b in (0, 1):
                where = at[2 * p + b]
                k_of, word = where // 32, jnp.left_shift(jnp.ones_like(where), where % 32)
                for k in range(16):
                    words[p, pl.ds(2 * k + b, 1), :] = jnp.sum(
                        jnp.where(k_of == k, word, 0), axis=0, keepdims=True)
            return carry

        lax.fori_loop(0, 3, band_words, 0)

    def kept_mask(words, c):
        word = words[...].reshape(LOW, 224)
        upper = (word // 256).astype(f32).astype(jnp.bfloat16)
        lower = (word % 256).astype(f32).astype(jnp.bfloat16)
        block = lax.broadcasted_iota(jnp.int32, (224, 128), 0)
        block_of = c * 8 + lax.broadcasted_iota(jnp.int32, (224, 128), 1) // 16
        spread = (block == block_of).astype(f32).astype(jnp.bfloat16)
        high = jnp.dot(upper, spread, preferred_element_type=f32)
        low = jnp.dot(lower, spread, preferred_element_type=f32)
        return jnp.right_shift((high * 256.0 + low).astype(jnp.int32), lane) & 1

    def moves(masks):
        dot = functools.partial(jnp.dot, preferred_element_type=f32)
        place = 16 * row + lane
        to_go = []
        for kept_here in masks:
            flags = kept_here.astype(f32).astype(jnp.bfloat16)
            in_rows = dot(flags, same[...]).astype(jnp.bfloat16)
            count = dot(flags, before[...]) + dot(above[...], in_rows)
            to_go.append(jnp.where(kept_here == 1, 0, count.astype(jnp.int32)))
        taken = [jnp.zeros_like(m) for m in masks]
        given = [jnp.zeros_like(m) for m in masks]
        for step in range(7):
            there = place + (1 << step) < 256
            for n, now in enumerate(to_go):
                coming = jnp.where(there, from_later(now, step), 0)
                takes, gives = coming & (1 << step), now & (1 << step)
                taken[n], given[n] = taken[n] | takes, given[n] | gives
                to_go[n] = jnp.where(takes != 0, coming, jnp.where(gives != 0, 0, now))
        return taken, given

    def pack(lows, taken):
        for step in range(7):
            lows = [jnp.where(t & (1 << step) != 0, from_later(low, step), low) for low, t in zip(lows, taken)]
        return lows

    def unpack(lows, given):
        for step in reversed(range(7)):
            lows = [jnp.where(t & (1 << step) != 0, from_earlier(low, step), low) for low, t in zip(lows, given)]
        return lows

    def sib_copy(c, n):
        src, dst = ((stage_far, far), (stage, own))[n]
        return pltpu.make_async_remote_copy(
            src_ref=src.at[c % SLOTS], dst_ref=dst.at[c],
            send_sem=ss_sem.at[c % SLOTS, n], recv_sem=sr_sem.at[c, n],
            device_id=sibling, device_id_type=MESH)

    def z_copy(c, rows):
        return pltpu.make_async_remote_copy(
            src_ref=far.at[c, pl.ds(0, rows)], dst_ref=zrecv.at[c, pl.ds(0, rows)],
            send_sem=zs_sem.at[c], recv_sem=zr_sem.at[c],
            device_id=partner, device_id_type=MESH)

    def send_stage(c):
        pltpu.make_async_copy(pbuf.at[c % LOADS], pbuf.at[c % LOADS], p_sem.at[c % LOADS]).wait()
        for n in (0, 1):
            @pl.when(c >= SLOTS)
            def _():
                sib_copy(c, n).wait_send()
            value = pbuf[c % LOADS, n].astype(f32)
            if n == 0:
                stage_far[c % SLOTS, :ROWS] = value[:, :128]
                stage_far[c % SLOTS, ROWS:] = value[:, 128:]
            else:
                stage[c % SLOTS] = value
            sib_copy(c, n).start()

    def process(g, j, packed):
        c = 4 * g + j
        sib_copy(c, 0).wait_recv()
        mine_far = pbuf[c % LOADS, 2].astype(f32)
        chip = jnp.concatenate([far[c, :ROWS] + mine_far[:, :128], far[c, ROWS:] + mine_far[:, 128:]], axis=1)
        if not packed:
            far[c, :ROWS] = chip[:, :128]
            far[c, ROWS:] = chip[:, 128:]
            z_copy(c, HALF).start()
            cf[g, 1, j] = forward(chip)
        else:
            lefted = split_dot((left[0], left[1]), chip)
            righted = split_dot(lefted[:LOW], (right[0], right[1]))
            cf[g, 1, j] = righted[:, :128]
            far[c, :LOW] = lefted[LOW:, :128]
            far[c, LOW:ROWS] = lefted[LOW:, 128:]
            far[c, ROWS:ROWS + LOW] = righted[:, 128:]
        sib_copy(c, 1).wait_recv()
        load_mom(c).wait()
        own[c] = own[c] + pbuf[c % LOADS, 3].astype(f32) + decay_rate * mombuf[c]
        pl.when(c + LOADS < CHUNKS)(lambda: start_part(c + LOADS, None))
        cf[g, 0, j] = forward(own[c])

    def pack_pair(g, j):
        taken, _ = moves([kept_mask(words_far, 4 * g + j + n) for n in (0, 1)])
        lows = pack([cf[g, 1, j + n] for n in (0, 1)], taken)
        for n, low in enumerate(lows):
            c = 4 * g + j + n
            for p in range(3):
                far[c, ROWS + LOW + 24 * p:ROWS + LOW + 24 * p + 24] = low[32 * p:32 * p + 24]
            pl.when(c < EARLY)(lambda c=c: z_copy(c, PACKED).start())

    def rs_send(g):
        def one(k, carry):
            py, px, target = in_plane(k)
            pltpu.make_async_remote_copy(
                src_ref=cf.at[g, :, py, pl.ds(pl.multiple_of(px * PIECE, 8), PIECE)],
                dst_ref=rsr.at[g, k - 1],
                send_sem=rs_s.at[g], recv_sem=rs_r.at[g],
                device_id=target, device_id_type=MESH).start()
            return carry
        lax.fori_loop(1, 16, one, 0)

    send_stage(0)
    for copy in consts:
        copy.start()
    lax.fori_loop(1, LOADS, start_part, 0)
    lax.fori_loop(0, CHUNKS, start_rest, 0)
    for copy in consts:
        copy.wait()
    for whole, pair in ((left32, left), (right32, right), (left_t32, left_t), (right_t32, right_t)):
        high = whole[...].astype(jnp.bfloat16)
        pair[0] = high
        pair[1] = (whole[...] - high.astype(f32)).astype(jnp.bfloat16)

    def kept_copy():
        return pltpu.make_async_remote_copy(
            src_ref=keptb, dst_ref=kept_far, send_sem=k_sem.at[0], recv_sem=k_sem.at[1],
            device_id=along_z(jnp.where(z_lo == 1, 1, 3)), device_id_type=MESH)

    mine = pl.ds(pl.multiple_of(x * PIECE, 8), PIECE)

    def z3_copy(g, step):
        target = along_z(jnp.where(z_lo == 1, 1, 3)) if step == 0 else along_z(2)
        return pltpu.make_async_remote_copy(
            src_ref=red.at[g, 1 - step], dst_ref=z3r.at[g, step],
            send_sem=z3_s.at[g, step], recv_sem=z3_r.at[g, step],
            device_id=target, device_id_type=MESH)

    def sum_plane(g, carry):
        pltpu.make_async_copy(rsr.at[g], rsr.at[g], rs_r.at[g]).wait()
        for n in (0, 1):
            total = cf[g, n, y, mine]
            for k in range(15):
                total = total + rsr[g, k, n]
            red[g, n] = total
        z3_copy(g, 0).start()
        return carry

    def gather_chip(packed, g, carry):
        for j in range(4):
            @pl.when(4 * g + j + 1 < CHUNKS)
            def _():
                send_stage(4 * g + j + 1)
            process(g, j, packed)
            if packed and j % 2 == 1:
                pack_pair(g, j - 1)
        if not packed:
            @pl.when(g == 0)
            def _():
                meet_plane()
                kept_copy().start()
        rs_send(g)
        if packed:
            pl.when(g >= 2)(lambda: sum_plane(g - 2, None))
        return carry

    lax.fori_loop(0, RAW, functools.partial(gather_chip, False), 0)
    r, c = (lax.broadcasted_iota(jnp.int32, (128, 128), n) for n in (0, 1))
    same[...] = (r // 16 == c // 16).astype(f32).astype(jnp.bfloat16)
    before[...] = ((r // 16 == c // 16) & (r < c)).astype(f32).astype(jnp.bfloat16)
    r, c = (lax.broadcasted_iota(jnp.int32, (LOW, LOW), n) for n in (0, 1))
    above[...] = ((r // 32 == c // 32) & (r % 2 == c % 2) & (c < r)).astype(f32).astype(jnp.bfloat16)

    unpack_words(rowbits, keptb)

    def group_mask(g, carry):
        for j in range(4):
            mask[g, j] = kept_mask(rowbits, 4 * g + j).astype(f32)
        return carry

    def group_moves(g, carry):
        for pair in (0, 2):
            _, given = moves([mask[g, pair + n].astype(jnp.int32) for n in (0, 1)])
            for n in (0, 1):
                gives_of[g, pair + n] = given[n]
        return carry

    lax.fori_loop(0, GROUPS, group_mask, 0)
    lax.fori_loop(RAW, MOVES, group_moves, 0)
    kept_copy().wait_recv()
    unpack_words(words_far, kept_far)
    lax.fori_loop(RAW, GROUPS, functools.partial(gather_chip, True), 0)

    def moment_copy(c):
        return pltpu.make_async_copy(own.at[c], moment_out.at[0, :, columns(c)], om_sem.at[c])

    def finish_raw(g, carry):
        for j in range(4):
            c = 4 * g + j
            z_copy(c, HALF).wait_recv()
            moment = own[c] + jnp.concatenate([zrecv[c, :ROWS], zrecv[c, ROWS:]], axis=1)
            own[c] = moment - inverse(mask[g, j] * forward(moment))
            moment_copy(c).start()
        return carry

    def finish(g, carry):
        fill = jnp.zeros((8, 128), f32)
        for pair in (0, 2):
            kept_here = [mask[g, pair + n].astype(jnp.int32) for n in (0, 1)]
            given = [gives_of[g, pair + n] for n in (0, 1)]
            packed = []
            for n in (0, 1):
                c = 4 * g + pair + n
                z_copy(c, PACKED).wait_recv()
                top = ROWS + LOW
                packed.append(jnp.concatenate(
                    [zrecv[c, top:top + 24], fill, zrecv[c, top + 24:top + 48], fill, zrecv[c, top + 48:top + 72], fill],
                    axis=0))
            others = unpack(packed, given)
            for n in (0, 1):
                c = 4 * g + pair + n
                low = jnp.where(kept_here[n] == 1, -cf[g, 0, pair + n], others[n])
                wide = split_dot(jnp.concatenate([low, zrecv[c, ROWS:ROWS + LOW]], axis=1), (right_t[0], right_t[1]))
                high = jnp.concatenate([zrecv[c, :LOW], zrecv[c, LOW:ROWS]], axis=1)
                both = jnp.concatenate([wide, high], axis=0)
                own[c] = own[c] + split_dot((left_t[0], left_t[1]), both)
                moment_copy(c).start()
        return carry

    lax.fori_loop(GROUPS - 2, GROUPS, sum_plane, 0)
    lax.fori_loop(0, RAW, finish_raw, 0)

    def sum_pair(g, carry):
        z3_copy(g, 0).wait_recv()
        red[g, 0] = red[g, 0] + z3r[g, 0]
        z3_copy(g, 1).start()
        return carry

    lax.fori_loop(0, GROUPS, sum_pair, 0)

    def start_z(c, carry):
        z_copy(c, PACKED).start()
        return carry

    lax.fori_loop(EARLY, CHUNKS, start_z, 0)
    lax.fori_loop(RAW, AHEAD, finish, 0)

    def sum_z(g, carry):
        z3_copy(g, 1).wait_recv()
        mean[g, y, mine] = red[g, 0] + z3r[g, 1]

        def one(k, inner):
            target = in_plane(k)[2]
            pltpu.make_async_remote_copy(
                src_ref=mean.at[g, y, mine], dst_ref=mean.at[g, y, mine],
                send_sem=ag_s.at[g], recv_sem=ag_r.at[g],
                device_id=target, device_id_type=MESH).start()
            return inner
        lax.fori_loop(1, 16, one, 0)
        return carry

    lax.fori_loop(0, GROUPS, sum_z, 0)


    def agg_copy(c):
        return pltpu.make_async_copy(mombuf.at[c], agg_out.at[:, columns(c)], oa_sem.at[c])

    def new_weight_copy(c):
        return pltpu.make_async_copy(wbuf.at[c], weight_out.at[:, columns(c)], ow_sem.at[c])

    def expand_mean(g, carry):
        pltpu.make_async_copy(rsr.at[g, :, 0], rsr.at[g, :, 0], ag_r.at[g]).wait()
        for j in range(4):
            c = 4 * g + j
            load_weight(c).wait()
            agg = inverse(mask[g, j] * (mean[g, j] / 32.0))
            mombuf[c] = agg
            wbuf[c] = (wbuf[c].astype(f32) - step_rate * agg).astype(jnp.bfloat16)
            agg_copy(c).start()
            new_weight_copy(c).start()
        return carry

    lax.fori_loop(MOVES, GROUPS, group_moves, 0)
    lax.fori_loop(AHEAD, MIDDLE, finish, 0)
    lax.fori_loop(0, GROUPS, expand_mean, 0)

    lax.fori_loop(MIDDLE, GROUPS, finish, 0)

    for c in range(CHUNKS - SLOTS, CHUNKS):
        for n in (0, 1):
            sib_copy(c, n).wait_send()

    def drain_chunk(c, carry):
        agg_copy(c).wait()
        new_weight_copy(c).wait()
        moment_copy(c).wait()
        return carry

    def drain_group(g, carry):
        pltpu.make_async_copy(rsr.at[g], rsr.at[g], rs_s.at[g]).wait()
        pltpu.make_async_copy(rsr.at[g, :, 0], rsr.at[g, :, 0], ag_s.at[g]).wait()
        for step in (0, 1):
            z3_copy(g, step).wait_send()
        return carry

    lax.fori_loop(0, GROUPS, drain_group, 0)
    lax.fori_loop(0, CHUNKS, drain_chunk, 0)

    def drain_z(rows, c, carry):
        z_copy(c, rows).wait_send()
        return carry

    lax.fori_loop(0, 4 * RAW, functools.partial(drain_z, HALF), 0)
    lax.fori_loop(4 * RAW, CHUNKS, functools.partial(drain_z, PACKED), 0)
    kept_copy().wait_send()


def write_out(*refs):
    ins, outs, sem = refs[:3], refs[3:6], refs[6]
    copies = []
    for n, (src, dst) in enumerate(zip(ins, outs)):
        if n == 0:
            src, dst = src.at[0], dst.at[0]
        for b in range(6):
            rows = pl.ds(32 * b, 32)
            copies.append(pltpu.make_async_copy(src.at[rows], dst.at[rows], sem.at[b, n]))
    for copy in copies:
        copy.start()
    for copy in copies:
        copy.wait()


def per_device(partials, momentum, weight, kept):
    left, right, left_t, right_t = (jnp.asarray(t) for t in tables())
    f32, bf16, i32 = jnp.float32, jnp.bfloat16, jnp.int32
    dma = pltpu.SemaphoreType.DMA
    vmem = pltpu.VMEM
    hbm = pl.BlockSpec(memory_space=pl.ANY)
    results = pl.pallas_call(
        kernel,
        out_shape=(
            vmem((1, ROWS, QUARTER), f32),
            vmem((ROWS, QUARTER), f32),
            vmem((ROWS, QUARTER), bf16),
        ),
        in_specs=[hbm] * 8,
        out_specs=(hbm,) * 3,
        scratch_shapes=[
            vmem((LOADS, 4, ROWS, CHUNK), bf16),
            vmem((SLOTS, ROWS, CHUNK), f32),
            vmem((SLOTS, HALF, 128), f32),
            vmem((CHUNKS, ROWS, CHUNK), f32),
            vmem((CHUNKS, HALF, 128), f32),
            vmem((CHUNKS, HALF, 128), f32),
            vmem((CHUNKS, ROWS, CHUNK), f32),
            vmem((CHUNKS, ROWS, CHUNK), bf16),
            vmem((GROUPS, 2, 4, LOW, 128), f32),
            vmem((GROUPS, 15, 2, PIECE, 128), f32),
            vmem((GROUPS, 2, PIECE, 128), f32),
            vmem((GROUPS, 2, PIECE, 128), f32),
            vmem((GROUPS, 4, LOW, 128), f32),
            vmem((GROUPS, 4, LOW, 128), f32),
            vmem((6, 64, 224), i32),
            vmem((3, 32, 224), i32),
            vmem((6, 64, 224), i32),
            vmem((3, 32, 224), i32),
            vmem((GROUPS, 4, LOW, 128), i32),
            vmem((128, 128), bf16),
            vmem((128, 128), bf16),
            vmem((LOW, LOW), bf16),
            vmem((ROWS, ROWS), f32),
            vmem((256, 256), f32),
            vmem((ROWS, ROWS), f32),
            vmem((256, 256), f32),
            vmem((2, ROWS, ROWS), bf16),
            vmem((2, 256, 256), bf16),
            vmem((2, ROWS, ROWS), bf16),
            vmem((2, 256, 256), bf16),
            dma((5,)), dma((LOADS,)), dma((CHUNKS,)), dma((CHUNKS,)),
            dma((SLOTS, 2)), dma((CHUNKS, 2)), dma((CHUNKS,)), dma((CHUNKS,)),
            dma((GROUPS,)), dma((GROUPS,)), dma((GROUPS, 2)), dma((GROUPS, 2)), dma((GROUPS,)), dma((GROUPS,)),
            dma((CHUNKS,)), dma((CHUNKS,)), dma((CHUNKS,)),
            dma((2,)), pltpu.SemaphoreType.REGULAR, pltpu.SemaphoreType.REGULAR,
        ],
        compiler_params=pltpu.CompilerParams(
            collective_id=0, has_side_effects=True, vmem_limit_bytes=48 * 2 ** 20),
        cost_estimate=pl.CostEstimate(flops=8 * 10 ** 9, bytes_accessed=34 * 10 ** 6, transcendentals=0),
        name="compress_step",
    )(partials, momentum, weight, jnp.transpose(kept, (0, 2, 1)), left, right, left_t, right_t)
    return pl.pallas_call(
        write_out,
        out_shape=tuple(jax.ShapeDtypeStruct(r.shape, r.dtype) for r in results),
        in_specs=[hbm] * 3,
        out_specs=(hbm,) * 3,
        scratch_shapes=[dma((6, 3))],
        compiler_params=pltpu.CompilerParams(vmem_limit_bytes=2 ** 20),
        name="write_out",
    )(*(pltpu.with_memory_space_constraint(r, vmem) for r in results))


def solution(mesh):
    placed = (
        P("rep", "shard", None, None),
        P("rep", None, "shard"),
        P(None, "shard"),
        P(None, "shard", None),
    )
    return jax.shard_map(
        per_device,
        mesh=mesh,
        in_specs=placed,
        out_specs=(P("rep", None, "shard"), P(None, "shard"), P(None, "shard")),
        check_vma=False,
    )
```

```python
import functools

import jax
import jax.numpy as jnp
import numpy as np
from jax import lax
from jax.experimental import pallas as pl
from jax.experimental.pallas import tpu as pltpu
from jax.sharding import PartitionSpec as P

decay_rate = 0.9
step_rate = 0.5

MESH = pl.DeviceIdType.MESH
ROWS = 192
LOW = 96
CHUNK = 256
CHUNKS = 28
GROUPS = 7
QUARTER = CHUNK * CHUNKS
SLOTS = 8
LOADS = 16
PIECE = 24
MOVES = 4
AHEAD = 3
MIDDLE = 4
RAW = 2
HALF = 2 * ROWS
PACKED = 360
EARLY = 16


def tables():
    freq = np.arange(32, dtype=np.float64)[:, None]
    place = np.arange(32, dtype=np.float64)[None, :]
    dct = np.cos(np.pi * (2.0 * place + 1.0) * freq / 64.0) * np.sqrt(2.0 / 32.0)
    dct[0] *= np.sqrt(0.5)
    left = np.zeros((ROWS, ROWS))
    for band in range(6):
        for k in range(16):
            left[32 * (band // 2) + 2 * k + band % 2, 32 * band:32 * band + 32] = dct[k]
            left[LOW + 16 * band + k, 32 * band:32 * band + 32] = dct[16 + k]
    right = np.concatenate([np.kron(np.eye(8), dct[:16].T), np.kron(np.eye(8), dct[16:].T)], axis=1)
    return tuple(np.ascontiguousarray(t, dtype=np.float32) for t in (left, right, left.T, right.T))


def two_terms(v):
    high = v.astype(jnp.bfloat16)
    return high, (v - high.astype(jnp.float32)).astype(jnp.bfloat16)


def split_dot(a, b):
    a_high, a_rest = a if isinstance(a, tuple) else two_terms(a)
    b_high, b_rest = b if isinstance(b, tuple) else two_terms(b)
    rows = a_high.shape[0]
    dot = functools.partial(jnp.dot, preferred_element_type=jnp.float32)
    first = dot(jnp.concatenate([a_high, a_rest], axis=0), b_high)
    return first[:rows] + (first[rows:] + dot(a_high, b_rest))


def kernel(part, mom, wt, kept, left_in, right_in, left_t_in, right_t_in,
           moment_out, agg_out, weight_out,
           pbuf, stage, stage_far, own, far, zrecv, mombuf, wbuf, cf, rsr, red, z3r, mean, mask, keptb, rowbits,
           kept_far, words_far, gives_of, same, before, above,
           left32, right32, left_t32, right_t32, left, right, left_t, right_t,
           const_sem, p_sem, m_sem, w_sem, ss_sem, sr_sem, zs_sem, zr_sem,
           rs_s, rs_r, z3_s, z3_r, ag_s, ag_r, om_sem, oa_sem, ow_sem, k_sem, ready_sem, plane_sem):
    f32 = jnp.float32
    rep, shard = lax.axis_index("rep"), lax.axis_index("shard")
    plane, z_hi = rep // 2, rep % 2
    y, x = plane // 4, plane % 4
    z_lo, core = shard // 2, shard % 2
    z = z_hi * 2 + z_lo

    def in_plane(k):
        py, px = (y + k // 4) % 4, (x + k % 4) % 4
        return py, px, ((py * 4 + px) * 2 + z_hi, shard)

    def along_z(dz):
        other = (z + dz) % 4
        return (plane * 2 + other // 2, (other % 2) * 2 + core)

    sibling = (rep, z_lo * 2 + (1 - core))
    partner = (rep, (1 - z_lo) * 2 + core)
    quarters = ((1 - z_lo) * 2 + (1 - core), z_lo * 2 + (1 - core), (1 - z_lo) * 2 + core, shard)

    def load_part(c):
        return [
            pltpu.make_async_copy(
                part.at[0, 0, :, pl.ds(pl.multiple_of(q * QUARTER + c * CHUNK, CHUNK), CHUNK)],
                pbuf.at[c % LOADS, n], p_sem.at[c % LOADS])
            for n, q in enumerate(quarters)
        ]

    def columns(c):
        return pl.ds(pl.multiple_of(c * CHUNK, CHUNK), CHUNK)

    def load_mom(c):
        return pltpu.make_async_copy(mom.at[0, :, columns(c)], mombuf.at[c], m_sem.at[c])

    def load_weight(c):
        return pltpu.make_async_copy(wt.at[:, columns(c)], wbuf.at[c], w_sem.at[c])

    consts = [
        pltpu.make_async_copy(src, dst, const_sem.at[n])
        for n, (src, dst) in enumerate(
            ((left_in, left32), (right_in, right32), (left_t_in, left_t32), (right_t_in, right_t32), (kept, keptb)))
    ]

    def start_part(c, carry):
        for copy in load_part(c):
            copy.start()
        return carry

    def start_mom(c, carry):
        load_mom(c).start()
        return carry

    def start_weight(c, carry):
        load_weight(c).start()
        return carry

    barrier = pltpu.get_barrier_semaphore()
    leads = z_lo == core

    @pl.when(jnp.logical_not(leads))
    def _():
        for other in (sibling, partner):
            pl.semaphore_signal(barrier, inc=1, device_id=other, device_id_type=MESH)

    start_part(0, 0)

    @pl.when(leads)
    def _():
        pl.semaphore_wait(barrier, 2)
        for other in (sibling, partner):
            pl.semaphore_signal(ready_sem, inc=1, device_id=other, device_id_type=MESH)

    @pl.when(jnp.logical_not(leads))
    def _():
        pl.semaphore_wait(ready_sem, 2)

        def greet(k, carry):
            pl.semaphore_signal(barrier, inc=1, device_id=in_plane(k)[2], device_id_type=MESH)
            return carry

        lax.fori_loop(1, 16, greet, 0)
        pl.semaphore_signal(barrier, inc=1, device_id=along_z(2), device_id_type=MESH)

    def meet_plane():
        @pl.when(jnp.logical_not(leads))
        def _():
            pl.semaphore_wait(barrier, 16)
            pl.semaphore_signal(plane_sem, inc=1, device_id=sibling, device_id_type=MESH)

        @pl.when(leads)
        def _():
            pl.semaphore_wait(plane_sem, 1)

    def forward(block):
        lefted = split_dot((left[0, :LOW], left[1, :LOW]), block)
        return split_dot(lefted, (right[0, :, :128], right[1, :, :128]))

    def inverse(low):
        wide = split_dot(low, (right_t[0, :128], right_t[1, :128]))
        return split_dot((left_t[0, :, :LOW], left_t[1, :, :LOW]), wide)

    row = lax.broadcasted_iota(jnp.int32, (LOW, 128), 0) % 32 // 2
    lane = lax.broadcasted_iota(jnp.int32, (LOW, 128), 1) % 16

    def turn(v, shift, axis):
        return pltpu.roll(v, shift % v.shape[axis], axis)

    def from_later(v, step):
        if step >= 4:
            return turn(v, -(2 << (step - 4)), 0)
        far = 1 << step
        return jnp.where(lane + far < 16, turn(v, -far, 1), turn(turn(v, -2, 0), 16 - far, 1))

    def from_earlier(v, step):
        if step >= 4:
            return turn(v, 2 << (step - 4), 0)
        far = 1 << step
        return jnp.where(lane >= far, turn(v, far, 1), turn(turn(v, 2, 0), -(16 - far), 1))

    def unpack_words(words, at):
        def band_words(p, carry):
            for b in (0, 1):
                where = at[2 * p + b]
                k_of, word = where // 32, jnp.left_shift(jnp.ones_like(where), where % 32)
                for k in range(16):
                    words[p, pl.ds(2 * k + b, 1), :] = jnp.sum(
                        jnp.where(k_of == k, word, 0), axis=0, keepdims=True)
            return carry

        lax.fori_loop(0, 3, band_words, 0)

    def kept_mask(words, c):
        word = words[...].reshape(LOW, 224)
        upper = (word // 256).astype(f32).astype(jnp.bfloat16)
        lower = (word % 256).astype(f32).astype(jnp.bfloat16)
        block = lax.broadcasted_iota(jnp.int32, (224, 128), 0)
        block_of = c * 8 + lax.broadcasted_iota(jnp.int32, (224, 128), 1) // 16
        spread = (block == block_of).astype(f32).astype(jnp.bfloat16)
        high = jnp.dot(upper, spread, preferred_element_type=f32)
        low = jnp.dot(lower, spread, preferred_element_type=f32)
        return jnp.right_shift((high * 256.0 + low).astype(jnp.int32), lane) & 1

    def moves(masks):
        dot = functools.partial(jnp.dot, preferred_element_type=f32)
        place = 16 * row + lane
        to_go = []
        for kept_here in masks:
            flags = kept_here.astype(f32).astype(jnp.bfloat16)
            in_rows = dot(flags, same[...]).astype(jnp.bfloat16)
            count = dot(flags, before[...]) + dot(above[...], in_rows)
            to_go.append(jnp.where(kept_here == 1, 0, count.astype(jnp.int32)))
        taken = [jnp.zeros_like(m) for m in masks]
        given = [jnp.zeros_like(m) for m in masks]
        for step in range(7):
            there = place + (1 << step) < 256
            for n, now in enumerate(to_go):
                coming = jnp.where(there, from_later(now, step), 0)
                takes, gives = coming & (1 << step), now & (1 << step)
                taken[n], given[n] = taken[n] | takes, given[n] | gives
                to_go[n] = jnp.where(takes != 0, coming, jnp.where(gives != 0, 0, now))
        return taken, given

    def pack(lows, taken):
        for step in range(7):
            lows = [jnp.where(t & (1 << step) != 0, from_later(low, step), low) for low, t in zip(lows, taken)]
        return lows

    def unpack(lows, given):
        for step in reversed(range(7)):
            lows = [jnp.where(t & (1 << step) != 0, from_earlier(low, step), low) for low, t in zip(lows, given)]
        return lows

    def sib_copy(c, n):
        src, dst = ((stage_far, far), (stage, own))[n]
        return pltpu.make_async_remote_copy(
            src_ref=src.at[c % SLOTS], dst_ref=dst.at[c],
            send_sem=ss_sem.at[c % SLOTS, n], recv_sem=sr_sem.at[c, n],
            device_id=sibling, device_id_type=MESH)

    def z_copy(c, rows):
        return pltpu.make_async_remote_copy(
            src_ref=far.at[c, pl.ds(0, rows)], dst_ref=zrecv.at[c, pl.ds(0, rows)],
            send_sem=zs_sem.at[c], recv_sem=zr_sem.at[c],
            device_id=partner, device_id_type=MESH)

    def send_stage(c):
        pltpu.make_async_copy(pbuf.at[c % LOADS], pbuf.at[c % LOADS], p_sem.at[c % LOADS]).wait()
        for n in (0, 1):
            @pl.when(c >= SLOTS)
            def _():
                sib_copy(c, n).wait_send()
            value = pbuf[c % LOADS, n].astype(f32)
            if n == 0:
                stage_far[c % SLOTS, :ROWS] = value[:, :128]
                stage_far[c % SLOTS, ROWS:] = value[:, 128:]
            else:
                stage[c % SLOTS] = value
            sib_copy(c, n).start()

    def process(g, j, packed):
        c = 4 * g + j
        if not packed:
            pl.when(c > 0)(lambda: raw_send(c))
            cf[g, 1, j] = forward(jnp.concatenate([far[c, :ROWS], far[c, ROWS:]], axis=1))
        else:
            sib_copy(c, 0).wait_recv()
            mine_far = pbuf[c % LOADS, 2].astype(f32)
            chip = jnp.concatenate([far[c, :ROWS] + mine_far[:, :128], far[c, ROWS:] + mine_far[:, 128:]], axis=1)
            lefted = split_dot((left[0], left[1]), chip)
            righted = split_dot(lefted[:LOW], (right[0], right[1]))
            cf[g, 1, j] = righted[:, :128]
            far[c, :LOW] = lefted[LOW:, :128]
            far[c, LOW:ROWS] = lefted[LOW:, 128:]
            far[c, ROWS:ROWS + LOW] = righted[:, 128:]
        sib_copy(c, 1).wait_recv()
        load_mom(c).wait()
        own[c] = own[c] + pbuf[c % LOADS, 3].astype(f32) + decay_rate * mombuf[c]
        pl.when(c + LOADS < CHUNKS)(lambda: start_part(c + LOADS, None))
        cf[g, 0, j] = forward(own[c])

    def pack_pair(g, j):
        taken, _ = moves([kept_mask(words_far, 4 * g + j + n) for n in (0, 1)])
        lows = pack([cf[g, 1, j + n] for n in (0, 1)], taken)
        for n, low in enumerate(lows):
            c = 4 * g + j + n
            for p in range(3):
                far[c, ROWS + LOW + 24 * p:ROWS + LOW + 24 * p + 24] = low[32 * p:32 * p + 24]
            pl.when(c < EARLY)(lambda c=c: z_copy(c, PACKED).start())

    def rs_send(g):
        def one(k, carry):
            py, px, target = in_plane(k)
            pltpu.make_async_remote_copy(
                src_ref=cf.at[g, :, py, pl.ds(pl.multiple_of(px * PIECE, 8), PIECE)],
                dst_ref=rsr.at[g, k - 1],
                send_sem=rs_s.at[g], recv_sem=rs_r.at[g],
                device_id=target, device_id_type=MESH).start()
            return carry
        lax.fori_loop(1, 16, one, 0)

    def raw_send(c):
        sib_copy(c, 0).wait_recv()
        mine_far = pbuf[c % LOADS, 2].astype(f32)
        far[c, :ROWS] = far[c, :ROWS] + mine_far[:, :128]
        far[c, ROWS:] = far[c, ROWS:] + mine_far[:, 128:]
        z_copy(c, HALF).start()

    send_stage(0)
    start_part(1, 0)
    start_part(2, 0)
    for copy in consts:
        copy.start()
    raw_send(0)
    lax.fori_loop(3, LOADS, start_part, 0)
    lax.fori_loop(0, CHUNKS, start_mom, 0)
    for copy in consts:
        copy.wait()
    for whole, pair in ((left32, left), (right32, right), (left_t32, left_t), (right_t32, right_t)):
        high = whole[...].astype(jnp.bfloat16)
        pair[0] = high
        pair[1] = (whole[...] - high.astype(f32)).astype(jnp.bfloat16)

    def kept_copy():
        return pltpu.make_async_remote_copy(
            src_ref=keptb, dst_ref=kept_far, send_sem=k_sem.at[0], recv_sem=k_sem.at[1],
            device_id=along_z(jnp.where(z_lo == 1, 1, 3)), device_id_type=MESH)

    mine = pl.ds(pl.multiple_of(x * PIECE, 8), PIECE)

    def z3_copy(g, step):
        target = along_z(jnp.where(z_lo == 1, 1, 3)) if step == 0 else along_z(2)
        return pltpu.make_async_remote_copy(
            src_ref=red.at[g, 1 - step], dst_ref=z3r.at[g, step],
            send_sem=z3_s.at[g, step], recv_sem=z3_r.at[g, step],
            device_id=target, device_id_type=MESH)

    def sum_plane(g, carry):
        pltpu.make_async_copy(rsr.at[g], rsr.at[g], rs_r.at[g]).wait()
        for n in (0, 1):
            total = cf[g, n, y, mine]
            for k in range(15):
                total = total + rsr[g, k, n]
            red[g, n] = total
        z3_copy(g, 0).start()
        return carry

    def gather_chip(packed, g, carry):
        for j in range(4):
            @pl.when(4 * g + j + 1 < CHUNKS)
            def _():
                send_stage(4 * g + j + 1)
            process(g, j, packed)
            if packed and j % 2 == 1:
                pack_pair(g, j - 1)
        if not packed:
            @pl.when(g == 0)
            def _():
                meet_plane()
                kept_copy().start()
        rs_send(g)
        if packed:
            pl.when(g >= 2)(lambda: sum_plane(g - 2, None))
        return carry

    lax.fori_loop(0, RAW, functools.partial(gather_chip, False), 0)
    r, c = (lax.broadcasted_iota(jnp.int32, (128, 128), n) for n in (0, 1))
    same[...] = (r // 16 == c // 16).astype(f32).astype(jnp.bfloat16)
    before[...] = ((r // 16 == c // 16) & (r < c)).astype(f32).astype(jnp.bfloat16)
    r, c = (lax.broadcasted_iota(jnp.int32, (LOW, LOW), n) for n in (0, 1))
    above[...] = ((r // 32 == c // 32) & (r % 2 == c % 2) & (c < r)).astype(f32).astype(jnp.bfloat16)

    unpack_words(rowbits, keptb)

    def group_mask(g, carry):
        for j in range(4):
            mask[g, j] = kept_mask(rowbits, 4 * g + j).astype(f32)
        return carry

    def group_moves(g, carry):
        for pair in (0, 2):
            _, given = moves([mask[g, pair + n].astype(jnp.int32) for n in (0, 1)])
            for n in (0, 1):
                gives_of[g, pair + n] = given[n]
        return carry

    lax.fori_loop(0, CHUNKS, start_weight, 0)
    lax.fori_loop(0, GROUPS, group_mask, 0)
    lax.fori_loop(RAW, MOVES, group_moves, 0)
    kept_copy().wait_recv()
    unpack_words(words_far, kept_far)
    lax.fori_loop(RAW, GROUPS, functools.partial(gather_chip, True), 0)

    def moment_copy(c):
        return pltpu.make_async_copy(own.at[c], moment_out.at[0, :, columns(c)], om_sem.at[c])

    def finish_raw(g, carry):
        for j in range(4):
            c = 4 * g + j
            z_copy(c, HALF).wait_recv()
            moment = own[c] + jnp.concatenate([zrecv[c, :ROWS], zrecv[c, ROWS:]], axis=1)
            own[c] = moment - inverse(mask[g, j] * forward(moment))
            moment_copy(c).start()
        return carry

    def finish(g, carry, sets=((0, 1), (2, 3))):
        fill = jnp.zeros((8, 128), f32)
        for js in sets:
            kept_here = [mask[g, j].astype(jnp.int32) for j in js]
            given = [gives_of[g, j] for j in js]
            packed = []
            for j in js:
                c = 4 * g + j
                z_copy(c, PACKED).wait_recv()
                top = ROWS + LOW
                packed.append(jnp.concatenate(
                    [zrecv[c, top:top + 24], fill, zrecv[c, top + 24:top + 48], fill, zrecv[c, top + 48:top + 72], fill],
                    axis=0))
            others = unpack(packed, given)
            for n, j in enumerate(js):
                c = 4 * g + j
                low = jnp.where(kept_here[n] == 1, -cf[g, 0, j], others[n])
                wide = split_dot(jnp.concatenate([low, zrecv[c, ROWS:ROWS + LOW]], axis=1), (right_t[0], right_t[1]))
                high = jnp.concatenate([zrecv[c, :LOW], zrecv[c, LOW:ROWS]], axis=1)
                both = jnp.concatenate([wide, high], axis=0)
                own[c] = own[c] + split_dot((left_t[0], left_t[1]), both)
                moment_copy(c).start()
        return carry

    lax.fori_loop(GROUPS - 2, GROUPS, sum_plane, 0)
    lax.fori_loop(0, 1, finish_raw, 0)

    def sum_pair(g, carry):
        z3_copy(g, 0).wait_recv()
        red[g, 0] = red[g, 0] + z3r[g, 0]
        z3_copy(g, 1).start()
        return carry

    lax.fori_loop(0, GROUPS, sum_pair, 0)

    def start_z(c, carry):
        z_copy(c, PACKED).start()
        return carry

    lax.fori_loop(EARLY, CHUNKS, start_z, 0)
    lax.fori_loop(1, RAW, finish_raw, 0)
    lax.fori_loop(RAW, AHEAD, finish, 0)

    def sum_z(g, carry):
        z3_copy(g, 1).wait_recv()
        mean[g, y, mine] = red[g, 0] + z3r[g, 1]

        def one(k, inner):
            target = in_plane(k)[2]
            pltpu.make_async_remote_copy(
                src_ref=mean.at[g, y, mine], dst_ref=mean.at[g, y, mine],
                send_sem=ag_s.at[g], recv_sem=ag_r.at[g],
                device_id=target, device_id_type=MESH).start()
            return inner
        lax.fori_loop(1, 16, one, 0)
        return carry

    lax.fori_loop(0, GROUPS, sum_z, 0)


    def agg_copy(c):
        return pltpu.make_async_copy(mombuf.at[c], agg_out.at[:, columns(c)], oa_sem.at[c])

    def new_weight_copy(c):
        return pltpu.make_async_copy(wbuf.at[c], weight_out.at[:, columns(c)], ow_sem.at[c])

    def expand_mean(g, carry):
        pltpu.make_async_copy(rsr.at[g, :, 0], rsr.at[g, :, 0], ag_r.at[g]).wait()
        for j in range(4):
            c = 4 * g + j
            load_weight(c).wait()
            agg = inverse(mask[g, j] * (mean[g, j] / 32.0))
            mombuf[c] = agg
            wbuf[c] = (wbuf[c].astype(f32) - step_rate * agg).astype(jnp.bfloat16)
            agg_copy(c).start()
            new_weight_copy(c).start()
        return carry

    lax.fori_loop(MOVES, GROUPS, group_moves, 0)
    lax.fori_loop(AHEAD, MIDDLE, finish, 0)
    lax.fori_loop(0, GROUPS, expand_mean, 0)

    lax.fori_loop(MIDDLE, GROUPS - 1, finish, 0)

    def drain_sib(c, carry):
        for n in (0, 1):
            sib_copy(c, n).wait_send()
        return carry

    def drain_agg(c, carry):
        agg_copy(c).wait()
        new_weight_copy(c).wait()
        return carry

    def drain_group(g, carry):
        pltpu.make_async_copy(rsr.at[g], rsr.at[g], rs_s.at[g]).wait()
        pltpu.make_async_copy(rsr.at[g, :, 0], rsr.at[g, :, 0], ag_s.at[g]).wait()
        for step in (0, 1):
            z3_copy(g, step).wait_send()
        return carry

    def drain_moment(rows, c, carry):
        z_copy(c, rows).wait_send()
        moment_copy(c).wait()
        return carry

    kept_copy().wait_send()
    lax.fori_loop(CHUNKS - SLOTS, CHUNKS, drain_sib, 0)
    lax.fori_loop(0, GROUPS, drain_group, 0)
    lax.fori_loop(0, CHUNKS, drain_agg, 0)
    lax.fori_loop(0, 4 * RAW, functools.partial(drain_moment, HALF), 0)
    lax.fori_loop(4 * RAW, CHUNKS - 4, functools.partial(drain_moment, PACKED), 0)
    finish(GROUPS - 1, 0, ((0, 1), (2,), (3,)))
    lax.fori_loop(CHUNKS - 4, CHUNKS, functools.partial(drain_moment, PACKED), 0)


def write_out(*refs):
    ins, outs, sem = refs[:3], refs[3:6], refs[6]
    copies = []
    for n, (src, dst) in enumerate(zip(ins, outs)):
        if n == 0:
            src, dst = src.at[0], dst.at[0]
        for b in range(6):
            rows = pl.ds(32 * b, 32)
            copies.append(pltpu.make_async_copy(src.at[rows], dst.at[rows], sem.at[b, n]))
    for copy in copies:
        copy.start()
    for copy in copies:
        copy.wait()


def per_device(partials, momentum, weight, kept):
    left, right, left_t, right_t = (jnp.asarray(t) for t in tables())
    f32, bf16, i32 = jnp.float32, jnp.bfloat16, jnp.int32
    dma = pltpu.SemaphoreType.DMA
    vmem = pltpu.VMEM
    hbm = pl.BlockSpec(memory_space=pl.ANY)
    results = pl.pallas_call(
        kernel,
        out_shape=(
            vmem((1, ROWS, QUARTER), f32),
            vmem((ROWS, QUARTER), f32),
            vmem((ROWS, QUARTER), bf16),
        ),
        in_specs=[hbm] * 8,
        out_specs=(hbm,) * 3,
        scratch_shapes=[
            vmem((LOADS, 4, ROWS, CHUNK), bf16),
            vmem((SLOTS, ROWS, CHUNK), f32),
            vmem((SLOTS, HALF, 128), f32),
            vmem((CHUNKS, ROWS, CHUNK), f32),
            vmem((CHUNKS, HALF, 128), f32),
            vmem((CHUNKS, HALF, 128), f32),
            vmem((CHUNKS, ROWS, CHUNK), f32),
            vmem((CHUNKS, ROWS, CHUNK), bf16),
            vmem((GROUPS, 2, 4, LOW, 128), f32),
            vmem((GROUPS, 15, 2, PIECE, 128), f32),
            vmem((GROUPS, 2, PIECE, 128), f32),
            vmem((GROUPS, 2, PIECE, 128), f32),
            vmem((GROUPS, 4, LOW, 128), f32),
            vmem((GROUPS, 4, LOW, 128), f32),
            vmem((6, 64, 224), i32),
            vmem((3, 32, 224), i32),
            vmem((6, 64, 224), i32),
            vmem((3, 32, 224), i32),
            vmem((GROUPS, 4, LOW, 128), i32),
            vmem((128, 128), bf16),
            vmem((128, 128), bf16),
            vmem((LOW, LOW), bf16),
            vmem((ROWS, ROWS), f32),
            vmem((256, 256), f32),
            vmem((ROWS, ROWS), f32),
            vmem((256, 256), f32),
            vmem((2, ROWS, ROWS), bf16),
            vmem((2, 256, 256), bf16),
            vmem((2, ROWS, ROWS), bf16),
            vmem((2, 256, 256), bf16),
            dma((5,)), dma((LOADS,)), dma((CHUNKS,)), dma((CHUNKS,)),
            dma((SLOTS, 2)), dma((CHUNKS, 2)), dma((CHUNKS,)), dma((CHUNKS,)),
            dma((GROUPS,)), dma((GROUPS,)), dma((GROUPS, 2)), dma((GROUPS, 2)), dma((GROUPS,)), dma((GROUPS,)),
            dma((CHUNKS,)), dma((CHUNKS,)), dma((CHUNKS,)),
            dma((2,)), pltpu.SemaphoreType.REGULAR, pltpu.SemaphoreType.REGULAR,
        ],
        compiler_params=pltpu.CompilerParams(
            collective_id=0, has_side_effects=True, vmem_limit_bytes=48 * 2 ** 20),
        cost_estimate=pl.CostEstimate(flops=8 * 10 ** 9, bytes_accessed=34 * 10 ** 6, transcendentals=0),
        name="compress_step",
    )(partials, momentum, weight, jnp.transpose(kept, (0, 2, 1)), left, right, left_t, right_t)
    return pl.pallas_call(
        write_out,
        out_shape=tuple(jax.ShapeDtypeStruct(r.shape, r.dtype) for r in results),
        in_specs=[hbm] * 3,
        out_specs=(hbm,) * 3,
        scratch_shapes=[dma((6, 3))],
        compiler_params=pltpu.CompilerParams(vmem_limit_bytes=2 ** 20),
        name="write_out",
    )(*(pltpu.with_memory_space_constraint(r, vmem) for r in results))


def solution(mesh):
    placed = (
        P("rep", "shard", None, None),
        P("rep", None, "shard"),
        P(None, "shard"),
        P(None, "shard", None),
    )
    return jax.shard_map(
        per_device,
        mesh=mesh,
        in_specs=placed,
        out_specs=(P("rep", None, "shard"), P(None, "shard"), P(None, "shard")),
        check_vma=False,
    )
```
